512 devices in a mesh: bx: 32 (over y_hi, z), by: 16 (over y_lo, x, core).
Axes of the slice: x: 4, y: 4 (y_hi: 2, y_lo: 2; y = y_hi * 2 + y_lo), z: 16, core: 2. Of those that a mesh axis runs over, the one named last changes fastest.
Arguments:
- polarization: float32 [3, 8, 1024, 2048], P(None, None, 'bx', 'by'), may hold values from -1.6 to 1.6
- alpha_field: float32 [8, 1024, 2048], P(None, 'bx', 'by'), may hold values from -1 to 1
- landau: float32 [3, 8], replicated, may hold values from 0.05 to 0.25
- stiffness: float32 [8], replicated, may hold values from 0.5 to 1.5
- permittivity: float32 [8], replicated, may hold values from 0.5 to 2
- interfaces: float32 [9], replicated, may hold values from 0.0002 to 0.0008
Outputs:
- polar_next: float32 [3, 8, 1024, 2048], P(None, None, 'bx', 'by')
- depol_field: float32 [3, 8, 1024, 2048], P(None, None, 'bx', 'by')
The draws below stay inside these ranges and needn't reach their ends.
All inputs are finite; a program needn't handle non-finite values.
Results may differ from the reference program's by a relative error of at most 0.0003.
Values sent between devices are 32-bit elements; how exact they have to be, the bound alone decides.
No kernel may reach another device: no remote copies, remote signals or barrier semaphores. Data moves between devices by JAX's collectives and lax.ppermute only.
A program may use at most 64 MiB of HBM per device.

```python
import math
import jax
import jax.numpy as jnp
from jax import lax

LAYERS = 8
STEPS = 2
NX = 1024
NY = 2048


def draw_polarization(key, part):
    return 0.5 * jax.random.truncated_normal(key, -3.2, 3.2, (3, LAYERS, NX, NY), jnp.float32)


def shard_levels(stream_key, shape, pieces, least, top_value):
    factor_of, own = 1.0, jax.random.fold_in(stream_key, 6)
    for axis_at, blocks in pieces:
        draws = jnp.exp(jax.random.uniform(jax.random.fold_in(own, axis_at), (blocks,), jnp.float32, least / len(pieces), top_value / len(pieces)))
        factor_of = factor_of * jnp.repeat(draws, shape[axis_at] // blocks).reshape([-1 if axis == axis_at else 1 for axis in range(len(shape))])
    return factor_of


def setup_inputs(seed: int = 0) -> dict:
    key_of = jax.random.split(jax.random.key(seed), 7)
    return {
        "polarization": draw_polarization(jax.random.fold_in(key_of[6], 71), 0),
        "alpha_field": jnp.clip(jax.random.uniform(key_of[1], (LAYERS, NX, NY), jnp.float32, -1.0, 1.0) * shard_levels(key_of[1], (LAYERS, NX, NY), ((1, 32), (2, 16)), -0.4, 0.0), -1.0, 1.0),
        "landau": jnp.clip(jax.random.uniform(key_of[2], (3, LAYERS), jnp.float32, 0.05, 0.25), 0.05, 0.25),
        "stiffness": jnp.clip(jax.random.uniform(key_of[3], (LAYERS,), jnp.float32, 0.5, 1.5), 0.5, 1.5),
        "permittivity": jnp.clip(jnp.exp(jax.random.uniform(key_of[4], (LAYERS,), jnp.float32, math.log(0.5), math.log(2.0))), 0.5, 2.0),
        "interfaces": jnp.clip(jnp.exp(jax.random.uniform(key_of[5], (LAYERS + 1,), jnp.float32, math.log(0.0002), math.log(0.0008))), 0.0002, 0.0008),
    }


step_size = 0.05


def shift_up(source, axis_no):
    upper_part = lax.slice_in_dim(source, 1, source.shape[axis_no], axis=axis_no)
    return jnp.concatenate([upper_part, jnp.zeros_like(lax.slice_in_dim(source, 0, 1, axis=axis_no))], axis=axis_no)


def shift_down(source, axis_no):
    lower_part = lax.slice_in_dim(source, 0, source.shape[axis_no] - 1, axis=axis_no)
    return jnp.concatenate([jnp.zeros_like(lax.slice_in_dim(source, 0, 1, axis=axis_no)), lower_part], axis=axis_no)


def central(source, axis_no):
    return 0.5 * (jnp.roll(source, -1, axis_no) - jnp.roll(source, 1, axis_no))


def depolarize(polar_now, permittivity, interfaces):
    charge = -(central(polar_now[0], 1) + central(polar_now[1], 2)
               + 0.5 * (shift_up(polar_now[2], 0) - shift_down(polar_now[2], 0)))
    spectrum = jnp.fft.fft2(charge)
    layers = charge.shape[0]
    grid_x = charge.shape[1]
    grid_y = charge.shape[2]
    wave_x = jnp.sin(jnp.pi * jnp.arange(grid_x).astype(jnp.float32) / grid_x)
    wave_y = jnp.sin(jnp.pi * jnp.arange(grid_y).astype(jnp.float32) / grid_y)
    lateral = 4.0 * wave_x[:, None] ** 2 + 4.0 * wave_y[None, :] ** 2
    ratios = []
    primes = []
    for layer_no in range(layers):
        diagonal = permittivity[layer_no] * lateral + interfaces[layer_no] + interfaces[layer_no + 1]
        source = spectrum[layer_no]
        if layer_no == 0:
            pivot_now = diagonal
            primed = source / pivot_now
        else:
            pivot_now = diagonal - interfaces[layer_no] * ratios[-1]
            primed = (source + interfaces[layer_no] * primes[-1]) / pivot_now
        primes.append(primed)
        ratios.append(interfaces[layer_no + 1] / pivot_now)
    values = [primes[-1]]
    for layer_no in range(layers - 2, -1, -1):
        values.insert(0, primes[layer_no] + ratios[layer_no] * values[0])
    potential = jnp.real(jnp.fft.ifft2(jnp.stack(values)))
    along_x = -0.5 * (jnp.roll(potential, -1, 1) - jnp.roll(potential, 1, 1))
    along_y = -0.5 * (jnp.roll(potential, -1, 2) - jnp.roll(potential, 1, 2))
    along_z = -0.5 * (shift_up(potential, 0) - shift_down(potential, 0))
    return jnp.stack([along_x, along_y, along_z])


def evolve(centre, alpha_field, landau, stiffness, field_now):
    squares = centre * centre
    total = squares[0] + squares[1] + squares[2]
    quartic = landau[0][None, :, None, None]
    mixed = landau[1][None, :, None, None]
    sextic = landau[2][None, :, None, None]
    kappa = stiffness[None, :, None, None]
    lateral = (jnp.roll(centre, -1, 2) + jnp.roll(centre, 1, 2) + jnp.roll(centre, -1, 3)
               + jnp.roll(centre, 1, 3) - 4.0 * centre)
    vertical = shift_up(centre, 1) + shift_down(centre, 1) - 2.0 * centre
    drive = (2.0 * alpha_field[None] * centre + 4.0 * quartic * centre * squares
             + 2.0 * mixed * centre * (total[None] - squares) + 6.0 * sextic * centre * squares * squares)
    smooth = kappa * (lateral + vertical)
    return centre - step_size * (drive - smooth - field_now)


def reference(polarization, alpha_field, landau, stiffness, permittivity, interfaces):
    polar_now = polarization
    field_now = jnp.zeros_like(polarization)
    for step_no in range(STEPS):
        field_now = depolarize(polar_now, permittivity, interfaces)
        polar_now = evolve(polar_now, alpha_field, landau, stiffness, field_now)
    return polar_now, field_now
```

```python
import functools

import jax
import jax.numpy as jnp
import ml_dtypes
import numpy as np
from jax import lax
from jax.experimental import pallas as pl
from jax.experimental.pallas import tpu as pltpu
from jax.sharding import PartitionSpec as P

DT = 0.05
NB = 16
LANES = 128
ROWS = 32
LAYERS = 8
SLOT = 72
BACK = 40
F32 = jnp.float32
BF16 = jnp.bfloat16
PARAMS = pltpu.CompilerParams(vmem_limit_bytes=48 * 1024 * 1024)


def split_table(table):
    high = table.astype(ml_dtypes.bfloat16)
    low = (table - high.astype(np.float64)).astype(ml_dtypes.bfloat16)
    return high, low


def tables_y():
    n = NB * LANES
    t = np.arange(LANES)
    k = np.arange(LANES)
    ang = 2 * np.pi * np.outer(k, t) / LANES
    c, s = np.cos(ang), np.sin(ang)
    fwd = np.block([[c, s], [-s, c]])
    inv = np.block([[c.T, -s.T], [s.T, c.T]]) * (2.0 / n)
    fwd0 = np.zeros((256, 256))
    inv0 = np.zeros((256, 256))
    for i in range(LANES):
        m = i if i <= 64 else i - 64
        wave = np.cos(2 * np.pi * m * t / LANES) if i <= 64 else np.sin(2 * np.pi * m * t / LANES)
        fwd0[i, :LANES] = wave
        inv0[:LANES, i] = wave * ((1.0 if i in (0, 64) else 2.0) / n)
    for i in range(64):
        th = 2 * np.pi * (8 + 16 * i) * t / n
        fwd0[128 + i, LANES:] = np.cos(th)
        fwd0[192 + i, LANES:] = -np.sin(th)
        inv0[LANES:, 128 + i] = np.cos(th) * (2.0 / n)
        inv0[LANES:, 192 + i] = -np.sin(th) * (2.0 / n)
    tw = np.zeros((16, LANES), np.float32)
    for j in range(8):
        tw[j] = np.cos(2 * np.pi * j * t / n)
        tw[8 + j] = np.sin(2 * np.pi * j * t / n)
    return fwd, fwd0, inv, inv0, tw


def tables_x(nx):
    half = nx // 2
    pos = np.arange(half)
    freq = []
    rows = []
    scale = np.sqrt(2.0 / nx)
    for k in range(0, half + 1, 2):
        w = np.cos(2 * np.pi * k * pos / nx)
        rows.append(w * (np.sqrt(1.0 / nx) if k in (0, half) else scale))
        freq.append(k)
    for k in range(2, half, 2):
        rows.append(np.sin(2 * np.pi * k * pos / nx) * scale)
        freq.append(k)
    for k in range(1, half, 2):
        rows.append(np.cos(2 * np.pi * k * pos / nx) * scale)
        freq.append(k)
    for k in range(1, half, 2):
        rows.append(np.sin(2 * np.pi * k * pos / nx) * scale)
        freq.append(k)
    table = np.stack(rows)
    order = np.array(
        [bx * ROWS + xl * NB + by for xl in range(2) for bx in range(half // ROWS) for by in range(NB)]
    )
    table = table[:, order]
    freq = np.array(freq)
    lam = np.zeros((8, nx), np.float32)
    lam[0] = 4 * np.sin(np.pi * freq / nx) ** 2
    lam[1] = np.sin(2 * np.pi * freq / nx) ** 2
    return table, lam


def split(value):
    high = value.astype(BF16)
    return high, (value - high.astype(F32)).astype(BF16)


def dot(a, b):
    return lax.dot_general(a, b, (((1,), (0,)), ((), ())), preferred_element_type=F32)


def dot_t(a, b):
    return lax.dot_general(a, b, (((1,), (1,)), ((), ())), preferred_element_type=F32)


def shift(value, by):
    n = value.shape[1]
    return pltpu.roll(value, by % n, axis=1)


def pack(tile):
    lane = lax.broadcasted_iota(jnp.int32, tile.shape, 1)
    edge = jnp.where((lane < 2) | (lane >= 126), tile, 0.0)
    return jnp.sum(pltpu.roll(edge, 0, axis=1, stride=4, stride_axis=0), axis=0, keepdims=True)


def unpack(row):
    value = jnp.broadcast_to(row, (8, LANES))
    index = lax.broadcasted_iota(jnp.int32, (8, LANES), 0)
    for bit in (1, 2, 4):
        value = jnp.where(index // bit % 2 == 1, pltpu.roll(value, LANES - 4 * bit, axis=1), value)
    return jnp.concatenate(
        [value] + [pltpu.roll(value, LANES - 32 * t, axis=1) for t in range(1, 4)], axis=0
    )


def drive_of(value, alpha2, total, quartic, mixed, sextic):
    sq = value * value
    return value * (
        alpha2 + 4.0 * quartic * sq + 2.0 * mixed * (total - sq) + 6.0 * sextic * (sq * sq)
    )


def charge_kernel(p_ref, al_ref, lo_ref, hi_ref, first_ref, last_ref, landau, stiff, out_ref, px, nx, ws):
    lane = lax.broadcasted_iota(jnp.int32, (ROWS, LANES), 1)
    for c in range(3):
        for l in range(LAYERS):
            n = c * LAYERS + l
            px[n, 8:40, :] = p_ref[c, l]
            px[n, 7:8, :] = lo_ref[1, n : n + 1, :]
            px[n, 40:41, :] = hi_ref[0, n : n + 1, :]
    row = lax.broadcasted_iota(jnp.int32, (LAYERS, LANES), 0)

    def by_layer(get):
        value = jnp.full((LAYERS, LANES), get(0), F32)
        for l in range(1, LAYERS):
            value = jnp.where(row == l, get(l), value)
        return value

    quartic = by_layer(lambda l: landau[0, l])
    mixed = by_layer(lambda l: landau[1, l])
    sextic = by_layer(lambda l: landau[2, l])
    kappa = by_layer(lambda l: stiff[l])
    for ref, at, outer, inner, target in (
        (lo_ref, 1, lo_ref[0, 0:8, :], first_ref[0, 0:8, :], 7),
        (hi_ref, 0, hi_ref[1, 0:8, :], last_ref[1, 0:8, :], 40),
    ):
        p0, p1, p2 = ref[at, 0:8, :], ref[at, 8:16, :], ref[at, 16:24, :]
        total = p0 * p0 + p1 * p1 + p2 * p2
        drive = drive_of(p0, 2.0 * ref[at, 24:32, :], total, quartic, mixed, sextic)
        up = jnp.where(row == LAYERS - 1, 0.0, pltpu.roll(p0, LAYERS - 1, axis=0))
        down = jnp.where(row == 0, 0.0, pltpu.roll(p0, 1, axis=0))
        value = p0 - DT * (drive - kappa * (outer + inner + up + down - 6.0 * p0))
        for l in range(LAYERS):
            nx[l, target : target + 1, :] = value[l : l + 1, :]

    def layer(ref, c, l):
        return ref[c, l] if 0 <= l < LAYERS else jnp.zeros((ROWS, LANES), F32)

    n1 = []
    n2 = []
    for l in range(LAYERS):
        p = [p_ref[c, l] for c in range(3)]
        total = p[0] * p[0] + p[1] * p[1] + p[2] * p[2]
        alpha2 = 2.0 * al_ref[l]
        e = DT * stiff[l]
        for c in range(3):
            n = c * LAYERS + l
            drive = drive_of(p[c], alpha2, total, landau[0, l], landau[1, l], landau[2, l])
            lap = (
                px[n, 9:41, :]
                + px[n, 7:39, :]
                + layer(p_ref, c, l + 1)
                + layer(p_ref, c, l - 1)
                - 6.0 * p[c]
            )
            value = p[c] - DT * drive + e * lap
            if c == 0:
                nx[l, 8:40, :] = value
            elif c == 1:
                n1.append(value)
            else:
                n2.append(value)
    for l in range(LAYERS):
        e = DT * stiff[l]
        zero = jnp.zeros((ROWS, LANES), F32)
        dx = -0.5 * (px[l, 9:41, :] - px[l, 7:39, :])
        above, below = layer(p_ref, 2, l + 1), layer(p_ref, 2, l - 1)
        p1 = p_ref[1, l]
        fwd, bwd = shift(p1, -1), shift(p1, 1)
        one = dx - 0.5 * (above - below) - 0.5 * (fwd - bwd)
        wrap_one = jnp.where(lane == LANES - 1, -0.5 * fwd, jnp.where(lane == 0, 0.5 * bwd, 0.0))
        e_up = DT * stiff[l + 1] if l + 1 < LAYERS else 0.0
        e_dn = DT * stiff[l - 1] if l > 0 else 0.0
        ue = e * dx - 0.5 * (e_up * above - e_dn * below)
        un = -0.5 * (nx[l, 9:41, :] - nx[l, 7:39, :]) - 0.5 * (
            (n2[l + 1] if l + 1 < LAYERS else zero) - (n2[l - 1] if l > 0 else zero)
        )
        a = shift(ue - 0.5 * n1[l], -1)
        b = shift(ue + 0.5 * n1[l], 1)
        h = (0.5 * e) * p1
        c2, d2 = shift(h, -2), shift(h, 2)
        two = un + a + b - c2 + d2
        wrap_two = (
            jnp.where(lane == LANES - 1, a, 0.0)
            + jnp.where(lane == 0, b, 0.0)
            + jnp.where(lane >= LANES - 2, -c2, 0.0)
            + jnp.where(lane < 2, d2, 0.0)
        )
        for f, (whole, wrap) in enumerate(((one, wrap_one), (two, wrap_two))):
            main = whole - wrap
            for xl in range(2):
                r = f * 16 + xl * 8 + l
                out_ref[pl.ds(r, NB, stride=SLOT), :] = main[xl * NB : (xl + 1) * NB]
                ws[pl.ds(r, NB, stride=32), :] = wrap[xl * NB : (xl + 1) * NB]
    tail = jnp.concatenate(
        [pack(lo_ref[1]), pack(hi_ref[0]), jnp.zeros((SLOT - 67, LANES), F32)], axis=0
    )
    for l in range(24):
        px[l, 0:1, :] = pack(p_ref[l // LAYERS, l % LAYERS])
    edges = [px[l, 0:1, :] for l in range(24)] + [pack(al_ref[l]) for l in range(LAYERS)]
    edges = jnp.concatenate(edges, axis=0)
    for b in range(NB):
        base = b * SLOT
        out_ref[base + 32 : base + 64, :] = edges
        out_ref[base + 64 : base + 65, :] = pack(ws[b * 32 : (b + 1) * 32, :])
        out_ref[base + 65 : base + SLOT, :] = tail


def y_forward_kernel(in_ref, fh, fl, f0h, f0l, tw, out_ref, d_ref, o_ref):
    lane1 = lax.broadcasted_iota(jnp.int32, (1, LANES), 1)
    lane = lax.broadcasted_iota(jnp.int32, (ROWS, LANES), 1)
    g = []
    for b in range(NB):
        before = in_ref[((b - 1) % NB) * SLOT + 64 : ((b - 1) % NB) * SLOT + 65, :]
        after = in_ref[((b + 1) % NB) * SLOT + 64 : ((b + 1) % NB) * SLOT + 65, :]
        extra = unpack(jnp.where(lane1 % 4 < 2, before, after))
        g.append(
            in_ref[b * SLOT : b * SLOT + 32, :]
            + jnp.where((lane < 2) | (lane >= 126), extra, 0.0)
        )
    plus = {b: g[b] + g[NB - b] for b in range(1, 8)}
    minus = {b: g[b] - g[NB - b] for b in range(1, 8)}
    re, im = {}, {}
    for k in range(5):
        even = g[0] + g[8] if k % 2 == 0 else g[0] - g[8]
        odd = jnp.zeros_like(even)
        s_even, s_odd = jnp.zeros_like(even), jnp.zeros_like(even)
        for b in range(1, 8):
            c, s = np.cos(2 * np.pi * b * k / 16), np.sin(2 * np.pi * b * k / 16)
            tc = plus[b] * float(c) if abs(c) > 1e-9 else None
            ts = minus[b] * float(s) if abs(s) > 1e-9 else None
            if b % 2 == 0:
                even = even + tc if tc is not None else even
                s_even = s_even + ts if ts is not None else s_even
            else:
                odd = odd + tc if tc is not None else odd
                s_odd = s_odd + ts if ts is not None else s_odd
        re[k], re[8 - k] = even + odd, even - odd
        im[k], im[8 - k] = -(s_even + s_odd), s_even - s_odd
    d_ref[0:32, 0:LANES] = re[0]
    d_ref[0:32, LANES:256] = re[8]
    re[4] = re[4]
    for j in range(1, 8):
        c, s = tw[j : j + 1, :], tw[8 + j : 9 + j, :]
        d_ref[j * 32 : (j + 1) * 32, 0:LANES] = re[j] * c + im[j] * s
        d_ref[j * 32 : (j + 1) * 32, LANES:256] = im[j] * c - re[j] * s
    dh, dl = split(d_ref[...])
    o_ref[...] = dot_t(fh[...], dh) + dot_t(fh[...], dl) + dot_t(fl[...], dh)
    zero = dot_t(f0h[...], dh[0:128]) + dot_t(f0h[...], dl[0:128]) + dot_t(f0l[...], dh[0:128])
    wide = lax.broadcasted_iota(jnp.int32, (256, LANES), 1)
    o_ref[:, 0:LANES] = jnp.where(wide < 32, zero, o_ref[:, 0:LANES])
    lane64 = lax.broadcasted_iota(jnp.int32, (64, LANES), 1)
    for j in range(8):
        t, at = j // 4, j % 4
        value = None
        for q in range(4):
            piece = o_ref[q * 64 : (q + 1) * 64, t * LANES : (t + 1) * LANES]
            if q != at:
                piece = shift(piece, (q - at) * 32)
            value = piece if value is None else jnp.where(lane64 // 32 == q, piece, value)
        out_ref[j * 64 : (j + 1) * 64, :] = value


def x_kernel(in_ref, th, tl, uh, ul, lam, eps, iface, out_ref, zs, ys):
    n = in_ref.shape[0]
    half = n // 2
    top, low = in_ref[0:half, :], in_ref[half:n, :]
    for part, value in enumerate((top + low, top - low)):
        high, rest = split(value)
        both = jnp.concatenate([high, rest], axis=1)
        for chunk in range(n // 256):
            r0 = part * n + chunk * 256
            acc = []
            for xl in range(2):
                cols = slice(xl * half, (xl + 1) * half)
                wide = dot(th[r0 : r0 + 256, cols], both)
                acc.append(
                    wide[:, 0:LANES] + wide[:, LANES:256] + dot(tl[r0 : r0 + 256, cols], high)
                )
            turned = jnp.transpose(acc[0] + shift(acc[1], -8))
            zs[r0 : r0 + LANES, :] = turned[:, 0:LANES]
            zs[r0 + LANES : r0 + 256, :] = turned[:, LANES:256]
    dev = lax.axis_index("bx") * NB + lax.axis_index("by")
    j = dev // 64
    q = lax.broadcasted_iota(jnp.int32, (8, 1), 0) // 2
    s = q * 64 + dev % 64
    ky_j = j + 16 * (s % 128)
    ky_0 = jnp.where(s < 128, 16 * jnp.where(s <= 64, s, s - 64), 8 + 16 * (s % 64))
    ky = jnp.where(j == 0, ky_0, ky_j)
    full = NB * LANES
    ky = jnp.minimum(ky, full - ky).astype(F32)
    ky = jnp.broadcast_to(ky, (8, LANES))
    sin_half = jnp.sin(ky * (np.pi / full))
    lam_y = 4.0 * sin_half * sin_half
    sin_y = jnp.sin(jnp.minimum(ky, full // 2 - ky) * (2.0 * np.pi / full))
    slope_y = sin_y * sin_y
    second = lax.broadcasted_iota(jnp.int32, (8, LANES), 0) % 2 == 1
    for chunk in range(2 * n // LANES):
        cols = slice(chunk * LANES, (chunk + 1) * LANES)
        lateral = lam_y + lam[0:1, cols]
        slope = slope_y + lam[1:2, cols]
        inverse, ratio = [], []
        for l in range(LAYERS):
            pivot = eps[l] * lateral + (iface[l] + iface[l + 1])
            if l > 0:
                pivot = pivot - iface[l] * ratio[-1]
            inverse.append(1.0 / pivot)
            ratio.append(iface[l + 1] * inverse[-1])

        def solve(source):
            prime = []
            for l in range(LAYERS):
                value = source[l] + iface[l] * prime[-1] if l > 0 else source[l]
                prime.append(value * inverse[l])
            for l in range(LAYERS - 2, -1, -1):
                prime[l] = prime[l] + ratio[l] * prime[l + 1]
            return prime

        phi = solve([zs[pl.ds(chunk * LANES + l, 8, stride=16), :] for l in range(LAYERS)])
        first = [jnp.where(second, pltpu.roll(v, 1, axis=0), 0.0) for v in phi]
        zero = jnp.zeros_like(first[0])

        def dz(v):
            return [
                0.5 * ((v[l + 1] if l + 1 < LAYERS else zero) - (v[l - 1] if l > 0 else zero))
                for l in range(LAYERS)
            ]

        twice = dz(dz(first))
        more = solve([DT * (twice[l] - slope * first[l]) for l in range(LAYERS)])
        for l in range(LAYERS):
            value = phi[l] + more[l]
            ys[pl.ds(chunk * LANES + l, 8, stride=16), :] = value
            ys[pl.ds(chunk * LANES + 8 + l, 8, stride=16), :] = value
    lane = lax.broadcasted_iota(jnp.int32, (half, LANES), 1)
    odd_row = lane // 8 % 2 == 1
    pair = []
    for part in range(2):
        cols = slice(part * n, (part + 1) * n)
        high, rest = split(
            jnp.concatenate([ys[r : r + LANES, :] for r in range(part * n, (part + 1) * n, LANES)], axis=1)
        )
        both = jnp.concatenate([high, rest], axis=0)
        acc = []
        for xl in range(2):
            rows = slice(xl * half, (xl + 1) * half)
            wide = dot_t(uh[rows, cols], both)
            acc.append(wide[:, 0:LANES] + wide[:, LANES:256] + dot_t(ul[rows, cols], high))
        pair.append(jnp.where(odd_row, acc[1], acc[0]))
    out_ref[0:half, :] = pair[0] + pair[1]
    out_ref[half:n, :] = pair[0] - pair[1]


def y_inverse_kernel(in_ref, gh, gl, g0h, g0l, tw, out_ref, o_ref):
    lane64 = lax.broadcasted_iota(jnp.int32, (64, LANES), 1)
    for t in range(2):
        for q in range(4):
            value = None
            for at in range(4):
                j = t * 4 + at
                piece = in_ref[j * 64 : (j + 1) * 64, :]
                if q != at:
                    piece = shift(piece, (at - q) * 32)
                value = piece if value is None else jnp.where(lane64 // 32 == at, piece, value)
            o_ref[q * 64 : (q + 1) * 64, t * LANES : (t + 1) * LANES] = value
    oh, ol = split(o_ref[...])
    o_ref[...] = dot(gh[...], oh) + dot(gh[...], ol) + dot(gl[...], oh)
    zero = (
        dot(g0h[...], oh[:, 0:LANES]) + dot(g0h[...], ol[:, 0:LANES]) + dot(g0l[...], oh[:, 0:LANES])
    )
    wide = lax.broadcasted_iota(jnp.int32, (256, LANES), 1)
    o_ref[:, 0:LANES] = jnp.where(wide < 32, zero, o_ref[:, 0:LANES])
    g = jnp.transpose(o_ref[...])
    hr, hi = {}, {}
    for j in range(1, 8):
        c, s = tw[j : j + 1, :], tw[8 + j : 9 + j, :]
        a, b = g[j * 32 : (j + 1) * 32, 0:LANES], g[j * 32 : (j + 1) * 32, LANES:256]
        hr[j] = a * c - b * s
        hi[j] = a * s + b * c
    g0, g8 = g[0:32, 0:LANES], g[0:32, LANES:256]
    out = {}
    for b in range(5):
        even = g0 + g8 if b % 2 == 0 else g0 - g8
        odd = jnp.zeros_like(even)
        s_even, s_odd = jnp.zeros_like(even), jnp.zeros_like(even)
        for j in range(1, 8):
            c, s = np.cos(2 * np.pi * b * j / 16), np.sin(2 * np.pi * b * j / 16)
            tc = hr[j] * float(c) if abs(c) > 1e-9 else None
            ts = hi[j] * float(s) if abs(s) > 1e-9 else None
            if j % 2 == 0:
                even = even + tc if tc is not None else even
                s_even = s_even + ts if ts is not None else s_even
            else:
                odd = odd + tc if tc is not None else odd
                s_odd = s_odd + ts if ts is not None else s_odd
        cos_b, sin_b = even + odd, s_even + s_odd
        cos_c, sin_c = even - odd, s_odd - s_even
        out[b] = cos_b - sin_b
        out[(NB - b) % NB] = cos_b + sin_b
        out[8 - b] = cos_c - sin_c
        out[8 + b] = cos_c + sin_c
    lane = lax.broadcasted_iota(jnp.int32, (ROWS, LANES), 1)
    blank = jnp.zeros((BACK - 33, LANES), F32)
    for b in range(NB):
        out_ref[b * BACK : b * BACK + 32, :] = out[b]
        border = jnp.where(lane < 2, out[(b + 1) % NB], out[(b - 1) % NB])
        out_ref[b * BACK + 32 : (b + 1) * BACK, :] = jnp.concatenate([pack(border), blank], axis=0)


def update_kernel(
    p_ref, al_ref, lo_ref, hi_ref, e_ref, phi_ref, flo_ref, fhi_ref, landau, stiff,
    out_ref, field_ref, px, fx, qx, ht,
):
    main, side = slice(0, LANES), slice(LANES, 2 * LANES)
    lane1 = lax.broadcasted_iota(jnp.int32, (ROWS, LANES), 1) % 4 < 2
    by = lax.axis_index("by")
    left, right = (by + NB - 1) % NB, (by + 1) % NB
    edges = jnp.where(lane1, e_ref[right, 32:64, :], e_ref[left, 32:64, :])
    corner = jnp.where(lane1[0:8], e_ref[right, 64:72, :], e_ref[left, 64:72, :])
    corner_lo, corner_hi = unpack(corner[1:2]), unpack(corner[2:3])
    for n in range(32):
        px[n, 8:40, main] = p_ref[n // LAYERS, n % LAYERS] if n < 24 else al_ref[n - 24]
        px[n, 8:40, side] = unpack(edges[n : n + 1])
        px[n, 6:7, main] = lo_ref[0, n : n + 1, :]
        px[n, 7:8, main] = lo_ref[1, n : n + 1, :]
        px[n, 40:41, main] = hi_ref[0, n : n + 1, :]
        px[n, 41:42, main] = hi_ref[1, n : n + 1, :]
        px[n, 7:8, side] = corner_lo[n : n + 1]
        px[n, 40:41, side] = corner_hi[n : n + 1]
        px[n, 6:7, side] = corner_lo[n : n + 1]
        px[n, 41:42, side] = corner_hi[n : n + 1]
    for src in range(NB):
        ht[src * 32 : (src + 1) * 32, :] = unpack(phi_ref[src * BACK + 32 : src * BACK + 33, :])
    far = [unpack(flo_ref[r, 32:33, :]) for r in range(2)]
    near = [unpack(fhi_ref[r, 32:33, :]) for r in range(2)]
    for f in range(2):
        for l in range(LAYERS):
            n = f * LAYERS + l
            for xl in range(2):
                r = f * 16 + xl * 8 + l
                rows = slice(8 + xl * NB, 8 + (xl + 1) * NB)
                fx[n, rows, main] = phi_ref[pl.ds(r, NB, stride=BACK), :]
                fx[n, rows, side] = ht[pl.ds(r, NB, stride=32), :]
            a, b = f * 16 + 8 + l, f * 16 + l
            for r in range(2):
                fx[n, 6 + r : 7 + r, main] = flo_ref[r, a : a + 1, :]
                fx[n, 6 + r : 7 + r, side] = far[r][a : a + 1]
                fx[n, 40 + r : 41 + r, main] = fhi_ref[r, b : b + 1, :]
                fx[n, 40 + r : 41 + r, side] = near[r][b : b + 1]

    def at(ref, base, l, rows):
        if 0 <= l < LAYERS:
            return ref[base + l, rows, :]
        return jnp.zeros((rows.stop - rows.start, ref.shape[2]), F32)

    ring = slice(7, 41)
    for l in range(LAYERS):
        p = [px[c * LAYERS + l, ring, :] for c in range(3)]
        total = p[0] * p[0] + p[1] * p[1] + p[2] * p[2]
        alpha2 = 2.0 * px[24 + l, ring, :]
        phi = fx[l, ring, :]
        slope = (
            fx[l, 8:42, :] - fx[l, 6:40, :],
            shift(phi, -1) - shift(phi, 1),
            at(fx, 0, l + 1, ring) - at(fx, 0, l - 1, ring),
        )
        for c in range(3):
            n = c * LAYERS + l
            drive = drive_of(p[c], alpha2, total, landau[0, l], landau[1, l], landau[2, l])
            lap = (
                px[n, 8:42, :] + px[n, 6:40, :] + shift(p[c], -1) + shift(p[c], 1)
                + at(px, c * LAYERS, l + 1, ring) + at(px, c * LAYERS, l - 1, ring)
                - 6.0 * p[c]
            )
            qx[n, ring, :] = p[c] - DT * (drive - stiff[l] * lap + 0.5 * slope[c])
    own = slice(8, 40)
    for l in range(LAYERS):
        wide = [qx[c * LAYERS + l, own, :] for c in range(3)]
        p = [w[:, main] for w in wide]
        total = p[0] * p[0] + p[1] * p[1] + p[2] * p[2]
        alpha2 = 2.0 * al_ref[l]
        phi = fx[LAYERS + l, own, :]
        up, down = at(fx, LAYERS, l + 1, own), at(fx, LAYERS, l - 1, own)
        field = (
            -0.5 * (fx[LAYERS + l, 9:41, main] - fx[LAYERS + l, 7:39, main]),
            -0.5 * (shift(phi, -1) - shift(phi, 1))[:, main],
            -0.5 * (up[:, main] - down[:, main]),
        )
        for c in range(3):
            n = c * LAYERS + l
            drive = drive_of(p[c], alpha2, total, landau[0, l], landau[1, l], landau[2, l])
            lap = (
                qx[n, 9:41, main] + qx[n, 7:39, main]
                + (shift(wide[c], -1) + shift(wide[c], 1))[:, main]
                + at(qx, c * LAYERS, l + 1, own)[:, main] + at(qx, c * LAYERS, l - 1, own)[:, main]
                - 6.0 * p[c]
            )
            out_ref[c, l] = p[c] - DT * (drive - stiff[l] * lap - field[c])
            field_ref[c, l] = field[c]


VMEM = pl.BlockSpec(memory_space=pltpu.VMEM)
SMEM = pl.BlockSpec(memory_space=pltpu.SMEM)


def call(kernel, shapes, specs, scratch, name):
    many = isinstance(shapes, list)
    return pl.pallas_call(
        kernel,
        out_shape=[jax.ShapeDtypeStruct(s, F32) for s in shapes]
        if many
        else jax.ShapeDtypeStruct(shapes, F32),
        in_specs=specs,
        out_specs=[VMEM] * len(shapes) if many else VMEM,
        scratch_shapes=[pltpu.VMEM(s, F32) for s in scratch],
        compiler_params=PARAMS,
        name=name,
    )


def shards(tabs, polarization, alpha_field, landau, stiffness, permittivity, interfaces):
    count = lax.axis_size("bx")
    devices = count * NB
    ahead = [(i, (i + 1) % count) for i in range(count)]
    behind = [(i, (i - 1) % count) for i in range(count)]
    cells = jnp.concatenate([polarization.reshape(24, ROWS, LANES), alpha_field], axis=0)
    first = jnp.swapaxes(cells[:, 0:2, :], 0, 1)
    last = jnp.swapaxes(cells[:, ROWS - 2 :, :], 0, 1)
    low = lax.ppermute(last, "bx", ahead)
    high = lax.ppermute(first, "bx", behind)
    sent = call(
        charge_kernel, (NB * SLOT, LANES), [VMEM] * 6 + [SMEM] * 2,
        [(24, 48, LANES), (LAYERS, 48, LANES), (NB * 32, LANES)], "charge",
    )(polarization, alpha_field, low, high, first, last, landau, stiffness)
    lines = lax.all_to_all(sent.reshape(NB, SLOT, LANES), "by", 0, 0, tiled=True)
    modes = call(
        y_forward_kernel, (devices, LANES), [VMEM] * 6, [(256, 256), (256, 256)], "y_forward"
    )(lines.reshape(NB * SLOT, LANES), *tabs["fwd"], *tabs["fwd0"], tabs["tw"])
    modes = lax.all_to_all(modes.reshape(devices, 1, LANES), ("bx", "by"), 0, 0, tiled=True)
    modes = call(
        x_kernel, (devices, LANES), [VMEM] * 6 + [SMEM] * 2,
        [(2 * devices, LANES), (2 * devices, LANES)], "x_solve",
    )(
        modes.reshape(devices, LANES), *tabs["x"], *tabs["xt"], tabs["lam"], permittivity, interfaces
    )
    modes = lax.all_to_all(modes.reshape(devices, 1, LANES), ("bx", "by"), 0, 0, tiled=True)
    sent = call(
        y_inverse_kernel, (NB * BACK, LANES), [VMEM] * 6, [(256, 256)], "y_inverse"
    )(modes.reshape(devices, LANES), *tabs["inv"], *tabs["inv0"], tabs["tw"])
    phi = lax.all_to_all(sent.reshape(NB, BACK, LANES), "by", 0, 0, tiled=True)
    phi_low = lax.ppermute(phi[NB - 2 :], "bx", ahead)
    phi_high = lax.ppermute(phi[:2], "bx", behind)
    return call(
        update_kernel,
        [(3, LAYERS, ROWS, LANES)] * 2,
        [VMEM] * 8 + [SMEM] * 2,
        [(32, 48, 256), (16, 48, 256), (24, 48, 256), (NB * 32, LANES)],
        "update",
    )(
        polarization, alpha_field, low, high, lines, phi.reshape(NB * BACK, LANES),
        phi_low, phi_high, landau, stiffness,
    )


def solution(mesh):
    fwd, fwd0, inv, inv0, tw = tables_y()
    table, lam = tables_x(mesh.shape["bx"] * ROWS)
    tabs = {
        "fwd": split_table(fwd), "fwd0": split_table(fwd0),
        "inv": split_table(inv), "inv0": split_table(inv0),
        "tw": tw, "x": split_table(table), "xt": split_table(table.T), "lam": lam,
    }
    return jax.shard_map(
        functools.partial(shards, tabs),
        mesh=mesh,
        in_specs=(P(None, None, "bx", "by"), P(None, "bx", "by"), P(), P(), P(), P()),
        out_specs=(P(None, None, "bx", "by"), P(None, None, "bx", "by")),
        check_vma=False,
    )
```

```python
import functools

import jax
import jax.numpy as jnp
import ml_dtypes
import numpy as np
from jax import lax
from jax.experimental import pallas as pl
from jax.experimental.pallas import tpu as pltpu
from jax.sharding import PartitionSpec as P

DT = 0.05
NB = 16
LANES = 128
ROWS = 32
LAYERS = 8
SLOT = 40
SHIFT = 2
F32 = jnp.float32
BF16 = jnp.bfloat16
PARAMS = pltpu.CompilerParams(vmem_limit_bytes=16 * 1024 * 1024)


def split_table(table):
    high = table.astype(ml_dtypes.bfloat16)
    low = (table - high.astype(np.float64)).astype(ml_dtypes.bfloat16)
    return high, low


def tables_y():
    n = NB * LANES
    t = np.arange(LANES)
    k = np.arange(LANES)
    ang = 2 * np.pi * np.outer(k, t) / LANES
    c, s = np.cos(ang), np.sin(ang)
    fwd = np.block([[c, s], [-s, c]])
    inv = np.block([[c.T, -s.T], [s.T, c.T]]) * (2.0 / n)
    fwd0 = np.zeros((256, 256))
    inv0 = np.zeros((256, 256))
    for i in range(LANES):
        m = i if i <= 64 else i - 64
        wave = np.cos(2 * np.pi * m * t / LANES) if i <= 64 else np.sin(2 * np.pi * m * t / LANES)
        fwd0[i, :LANES] = wave
        inv0[:LANES, i] = wave * ((1.0 if i in (0, 64) else 2.0) / n)
    for i in range(64):
        th = 2 * np.pi * (8 + 16 * i) * t / n
        fwd0[128 + i, LANES:] = np.cos(th)
        fwd0[192 + i, LANES:] = -np.sin(th)
        inv0[LANES:, 128 + i] = np.cos(th) * (2.0 / n)
        inv0[LANES:, 192 + i] = -np.sin(th) * (2.0 / n)
    tw = np.zeros((16, LANES), np.float32)
    for j in range(8):
        tw[j] = np.cos(2 * np.pi * j * t / n)
        tw[8 + j] = np.sin(2 * np.pi * j * t / n)
    return fwd, fwd0, inv, inv0, tw


def tables_x(nx, offset):
    half = nx // 2
    pos = np.array(
        [
            bx * ROWS + xl * NB + by + offset
            for xl in range(2)
            for bx in range(half // ROWS)
            for by in range(NB)
        ]
    )
    even, odd = list(range(0, half + 1, 2)), list(range(1, half, 2))
    kinds = [(k, 0) for k in even] + [(k, 1) for k in even[1:-1]] + [(k, 0) for k in odd] + [(k, 1) for k in odd]
    scale = np.sqrt(2.0 / nx)
    rows = []
    for k, kind in kinds:
        wave = (np.sin if kind else np.cos)(2 * np.pi * (k * pos % nx) / nx)
        rows.append(wave * (np.sqrt(1.0 / nx) if k in (0, half) else scale))
    freq = np.array([k for k, _ in kinds])
    lam = np.zeros((8, nx), np.float32)
    lam[0] = 4 * np.sin(np.pi * freq / nx) ** 2
    lam[1] = np.sin(2 * np.pi * freq / nx) ** 2
    return np.stack(rows), lam


def split(value):
    high = value.astype(BF16)
    return high, (value - high.astype(F32)).astype(BF16)


def dot(a, b):
    return lax.dot_general(a, b, (((1,), (0,)), ((), ())), preferred_element_type=F32)


def dot_t(a, b):
    return lax.dot_general(a, b, (((1,), (1,)), ((), ())), preferred_element_type=F32)


def shift(value, by):
    n = value.shape[1]
    return pltpu.roll(value, by % n, axis=1)


def pack(tile):
    lane = lax.broadcasted_iota(jnp.int32, tile.shape, 1)
    edge = jnp.where((lane < 2) | (lane >= 126), tile, 0.0)
    return jnp.sum(pltpu.roll(edge, 0, axis=1, stride=4, stride_axis=0), axis=0, keepdims=True)


def unpack(row):
    value = jnp.broadcast_to(row, (8, LANES))
    index = lax.broadcasted_iota(jnp.int32, (8, LANES), 0)
    for bit in (1, 2, 4):
        value = jnp.where(index // bit % 2 == 1, pltpu.roll(value, LANES - 4 * bit, axis=1), value)
    return jnp.concatenate(
        [value] + [pltpu.roll(value, LANES - 32 * t, axis=1) for t in range(1, 4)], axis=0
    )


def drive_of(value, alpha2, total, quartic, mixed, sextic):
    sq = value * value
    return value * (alpha2 + quartic * sq + mixed * (total - sq) + sextic * (sq * sq))


def coefficient(par, kind, l, width=LANES):
    return par[kind * LAYERS + l : kind * LAYERS + l + 1, 0:width]


def border_kernel(p_ref, al_ref, last_ref, first_ref, buf, sems):
    copies = [
        pltpu.make_async_copy(src.at[:, rows, :], buf.at[k, cells], sems.at[2 * k + m])
        for k, rows in enumerate((pl.ds(ROWS - 8, 8), pl.ds(0, 8)))
        for m, (src, cells) in enumerate(((p_ref, pl.ds(0, 24)), (al_ref, pl.ds(24, 8))))
    ]
    for copy in copies:
        copy.start()
    for copy in copies:
        copy.wait()
    for n in range(32):
        for r in range(4):
            last_ref[r * 32 + n : r * 32 + n + 1, :] = buf[0, n, 4 + r : 5 + r, :]
        for r in range(2):
            first_ref[r * 32 + n : r * 32 + n + 1, :] = buf[1, n, r : r + 1, :]


def charge_kernel(p_ref, al_ref, lo_ref, par, out_ref, px, nx, ws, eb):
    lane = lax.broadcasted_iota(jnp.int32, (ROWS, LANES), 1)
    for n in range(24):
        px[n * 40 + 8 : n * 40 + 40, :] = p_ref[n * ROWS : (n + 1) * ROWS, :]
    for l in range(LAYERS):
        px[(24 + l) * 40 + 8 : (24 + l) * 40 + 40, :] = al_ref[l * ROWS : (l + 1) * ROWS, :]
    for r in range(4):
        px[pl.ds(4 + r, 32, stride=40), :] = lo_ref[r * 32 : (r + 1) * 32, :]

    def at(ref, c, l, low, high):
        if 0 <= l < LAYERS:
            n = c * LAYERS + l
            return ref[n * 40 + low : n * 40 + high, :]
        return jnp.zeros((high - low, LANES), F32)

    for l in range(LAYERS):
        p = [at(px, c, l, 5, 39) for c in range(3)]
        total = p[0] * p[0] + p[1] * p[1] + p[2] * p[2]
        alpha2 = 2.0 * at(px, 3, l, 5, 39)
        e = coefficient(par, 3, l)
        landau = [coefficient(par, k, l) for k in range(3)]
        for c in range(3):
            drive = drive_of(p[c], alpha2, total, *landau)
            lap = (
                at(px, c, l, 6, 40) + at(px, c, l, 4, 38)
                + at(px, c, l + 1, 5, 39) + at(px, c, l - 1, 5, 39)
                - 6.0 * p[c]
            )
            n = c * LAYERS + l
            nx[n * 40 + 5 : n * 40 + 39, :] = p[c] - DT * drive + e * lap
    for l in range(LAYERS):
        e = coefficient(par, 3, l)
        dx = -0.5 * (at(px, 0, l, 7, 39) - at(px, 0, l, 5, 37))
        above, below = at(px, 2, l + 1, 6, 38), at(px, 2, l - 1, 6, 38)
        p1, n1 = at(px, 1, l, 6, 38), at(nx, 1, l, 6, 38)
        fwd, bwd = shift(p1, -1), shift(p1, 1)
        one = dx - 0.5 * (above - below) - 0.5 * (fwd - bwd)
        wrap_one = jnp.where(lane == LANES - 1, -0.5 * fwd, jnp.where(lane == 0, 0.5 * bwd, 0.0))
        e_up = coefficient(par, 3, l + 1) if l + 1 < LAYERS else 0.0
        e_dn = coefficient(par, 3, l - 1) if l > 0 else 0.0
        ue = e * dx - 0.5 * (e_up * above - e_dn * below)
        un = -0.5 * (at(nx, 0, l, 7, 39) - at(nx, 0, l, 5, 37)) - 0.5 * (
            at(nx, 2, l + 1, 6, 38) - at(nx, 2, l - 1, 6, 38)
        )
        a = shift(ue - 0.5 * n1, -1)
        b = shift(ue + 0.5 * n1, 1)
        h = (0.5 * e) * p1
        c2, d2 = shift(h, -2), shift(h, 2)
        two = un + a + b - c2 + d2
        wrap_two = (
            jnp.where(lane == LANES - 1, a, 0.0)
            + jnp.where(lane == 0, b, 0.0)
            + jnp.where(lane >= LANES - 2, -c2, 0.0)
            + jnp.where(lane < 2, d2, 0.0)
        )
        for f, (whole, wrap) in enumerate(((one, wrap_one), (two, wrap_two))):
            main = whole - wrap
            for xl in range(2):
                r = f * 16 + xl * 8 + l
                out_ref[pl.ds(r, NB, stride=SLOT), :] = main[xl * NB : (xl + 1) * NB]
                ws[pl.ds(r, NB, stride=32), :] = wrap[xl * NB : (xl + 1) * NB]
    for n in range(32):
        eb[n : n + 1, :] = pack(px[n * 40 + 8 : n * 40 + 40, :])
    eb[32:33, :] = pack(lo_ref[96:128, :])
    eb[33:48, :] = jnp.zeros((15, LANES), F32)
    blank = jnp.zeros((4, LANES), F32)
    for b in range(NB):
        out_ref[b * SLOT + 32 : (b + 1) * SLOT, :] = jnp.concatenate(
            [pack(ws[b * 32 : (b + 1) * 32, :]), eb[3 * b : 3 * b + 3, :], blank], axis=0
        )


def y_forward_kernel(in_ref, fh, fl, f0h, f0l, tw, hi_ref, out_ref, corner_ref, d_ref, o_ref):
    corner_ref[...] = jnp.concatenate([pack(hi_ref[0:32, :]), jnp.zeros((7, LANES), F32)], axis=0)
    lane1 = lax.broadcasted_iota(jnp.int32, (1, LANES), 1)
    lane = lax.broadcasted_iota(jnp.int32, (ROWS, LANES), 1)
    g = []
    for b in range(NB):
        before = in_ref[((b - 1) % NB) * SLOT + 32 : ((b - 1) % NB) * SLOT + 33, :]
        after = in_ref[((b + 1) % NB) * SLOT + 32 : ((b + 1) % NB) * SLOT + 33, :]
        extra = unpack(jnp.where(lane1 % 4 < 2, before, after))
        g.append(
            in_ref[b * SLOT : b * SLOT + 32, :]
            + jnp.where((lane < 2) | (lane >= 126), extra, 0.0)
        )
    plus = {b: g[b] + g[NB - b] for b in range(1, 8)}
    minus = {b: g[b] - g[NB - b] for b in range(1, 8)}
    re, im = {}, {}
    for k in range(5):
        even = g[0] + g[8] if k % 2 == 0 else g[0] - g[8]
        odd = jnp.zeros_like(even)
        s_even, s_odd = jnp.zeros_like(even), jnp.zeros_like(even)
        for b in range(1, 8):
            c, s = np.cos(2 * np.pi * b * k / 16), np.sin(2 * np.pi * b * k / 16)
            tc = plus[b] * float(c) if abs(c) > 1e-9 else None
            ts = minus[b] * float(s) if abs(s) > 1e-9 else None
            if b % 2 == 0:
                even = even + tc if tc is not None else even
                s_even = s_even + ts if ts is not None else s_even
            else:
                odd = odd + tc if tc is not None else odd
                s_odd = s_odd + ts if ts is not None else s_odd
        re[k], re[8 - k] = even + odd, even - odd
        im[k], im[8 - k] = -(s_even + s_odd), s_even - s_odd
    d_ref[0:32, 0:LANES] = re[0]
    d_ref[0:32, LANES:256] = re[8]
    for j in range(1, 8):
        c, s = tw[j : j + 1, :], tw[8 + j : 9 + j, :]
        d_ref[j * 32 : (j + 1) * 32, 0:LANES] = re[j] * c + im[j] * s
        d_ref[j * 32 : (j + 1) * 32, LANES:256] = im[j] * c - re[j] * s
    dh, dl = split(d_ref[...])
    o_ref[...] = dot_t(fh[...], dh) + dot_t(fh[...], dl) + dot_t(fl[...], dh)
    zero = dot_t(f0h[...], dh[0:128]) + dot_t(f0h[...], dl[0:128]) + dot_t(f0l[...], dh[0:128])
    wide = lax.broadcasted_iota(jnp.int32, (256, LANES), 1)
    o_ref[:, 0:LANES] = jnp.where(wide < 32, zero, o_ref[:, 0:LANES])
    lane64 = lax.broadcasted_iota(jnp.int32, (64, LANES), 1)
    for j in range(8):
        t, at = j // 4, j % 4
        value = None
        for q in range(4):
            piece = o_ref[q * 64 : (q + 1) * 64, t * LANES : (t + 1) * LANES]
            if q != at:
                piece = shift(piece, (q - at) * 32)
            value = piece if value is None else jnp.where(lane64 // 32 == q, piece, value)
        out_ref[j * 64 : (j + 1) * 64, :] = value


def x_kernel(in_ref, th, tl, uh, ul, lam, par, out_ref, zs, ys):
    n = in_ref.shape[0]
    half = n // 2
    top, low = in_ref[0:half, :], in_ref[half:n, :]
    for part, value in enumerate((top + low, top - low)):
        high, rest = split(value)
        both = jnp.concatenate([high, rest], axis=1)
        for chunk in range(n // 256):
            r0 = part * n + chunk * 256
            acc = []
            for xl in range(2):
                cols = slice(xl * half, (xl + 1) * half)
                wide = dot(th[r0 : r0 + 256, cols], both)
                acc.append(
                    wide[:, 0:LANES] + wide[:, LANES:256] + dot(tl[r0 : r0 + 256, cols], high)
                )
            turned = jnp.transpose(acc[0] + shift(acc[1], -8))
            zs[r0 : r0 + LANES, :] = turned[:, 0:LANES]
            zs[r0 + LANES : r0 + 256, :] = turned[:, LANES:256]
    dev = lax.axis_index("bx") * NB + lax.axis_index("by")
    j = dev // 64
    q = lax.broadcasted_iota(jnp.int32, (8, 1), 0) // 2
    s = q * 64 + dev % 64
    ky_j = j + 16 * (s % 128)
    ky_0 = jnp.where(s < 128, 16 * jnp.where(s <= 64, s, s - 64), 8 + 16 * (s % 64))
    ky = jnp.where(j == 0, ky_0, ky_j)
    full = NB * LANES
    ky = jnp.minimum(ky, full - ky).astype(F32)
    ky = jnp.broadcast_to(ky, (8, LANES))
    sin_half = jnp.sin(ky * (np.pi / full))
    lam_y = 4.0 * sin_half * sin_half
    sin_y = jnp.sin(jnp.minimum(ky, full // 2 - ky) * (2.0 * np.pi / full))
    slope_y = sin_y * sin_y
    second = lax.broadcasted_iota(jnp.int32, (8, LANES), 0) % 2 == 1
    eps = [coefficient(par, 4, l) for l in range(LAYERS)]
    iface = [coefficient(par, 5, l) for l in range(LAYERS + 1)]
    for chunk in range(2 * n // LANES):
        cols = slice(chunk * LANES, (chunk + 1) * LANES)
        lateral = lam_y + lam[0:1, cols]
        slope = slope_y + lam[1:2, cols]
        inverse, ratio = [], []
        for l in range(LAYERS):
            pivot = eps[l] * lateral + (iface[l] + iface[l + 1])
            if l > 0:
                pivot = pivot - iface[l] * ratio[-1]
            inverse.append(1.0 / pivot)
            ratio.append(iface[l + 1] * inverse[-1])

        def solve(source):
            prime = []
            for l in range(LAYERS):
                value = source[l] + iface[l] * prime[-1] if l > 0 else source[l]
                prime.append(value * inverse[l])
            for l in range(LAYERS - 2, -1, -1):
                prime[l] = prime[l] + ratio[l] * prime[l + 1]
            return prime

        phi = solve([zs[pl.ds(chunk * LANES + l, 8, stride=16), :] for l in range(LAYERS)])
        first = [jnp.where(second, pltpu.roll(v, 1, axis=0), 0.0) for v in phi]
        zero = jnp.zeros_like(first[0])

        def dz(v):
            return [
                0.5 * ((v[l + 1] if l + 1 < LAYERS else zero) - (v[l - 1] if l > 0 else zero))
                for l in range(LAYERS)
            ]

        twice = dz(dz(first))
        more = solve([DT * (twice[l] - slope * first[l]) for l in range(LAYERS)])
        for l in range(LAYERS):
            value = phi[l] + more[l]
            ys[pl.ds(chunk * LANES + l, 8, stride=16), :] = value
            ys[pl.ds(chunk * LANES + 8 + l, 8, stride=16), :] = value
    lane = lax.broadcasted_iota(jnp.int32, (half, LANES), 1)
    odd_row = lane // 8 % 2 == 1
    pair = []
    for part in range(2):
        cols = slice(part * n, (part + 1) * n)
        high, rest = split(
            jnp.concatenate([ys[r : r + LANES, :] for r in range(part * n, (part + 1) * n, LANES)], axis=1)
        )
        both = jnp.concatenate([high, rest], axis=0)
        acc = []
        for xl in range(2):
            rows = slice(xl * half, (xl + 1) * half)
            wide = dot_t(uh[rows, cols], both)
            acc.append(wide[:, 0:LANES] + wide[:, LANES:256] + dot_t(ul[rows, cols], high))
        pair.append(jnp.where(odd_row, acc[1], acc[0]))
    out_ref[0:half, :] = pair[0] + pair[1]
    out_ref[half:n, :] = pair[0] - pair[1]


def y_inverse_kernel(in_ref, gh, gl, g0h, g0l, tw, lines, corner_ref, out_ref, o_ref):
    lane64 = lax.broadcasted_iota(jnp.int32, (64, LANES), 1)
    for t in range(2):
        for q in range(4):
            value = None
            for at in range(4):
                j = t * 4 + at
                piece = in_ref[j * 64 : (j + 1) * 64, :]
                if q != at:
                    piece = shift(piece, (at - q) * 32)
                value = piece if value is None else jnp.where(lane64 // 32 == at, piece, value)
            o_ref[q * 64 : (q + 1) * 64, t * LANES : (t + 1) * LANES] = value
    oh, ol = split(o_ref[...])
    o_ref[...] = dot(gh[...], oh) + dot(gh[...], ol) + dot(gl[...], oh)
    zero = (
        dot(g0h[...], oh[:, 0:LANES]) + dot(g0h[...], ol[:, 0:LANES]) + dot(g0l[...], oh[:, 0:LANES])
    )
    wide = lax.broadcasted_iota(jnp.int32, (256, LANES), 1)
    o_ref[:, 0:LANES] = jnp.where(wide < 32, zero, o_ref[:, 0:LANES])
    g = jnp.transpose(o_ref[...])
    hr, hi = {}, {}
    for j in range(1, 8):
        c, s = tw[j : j + 1, :], tw[8 + j : 9 + j, :]
        a, b = g[j * 32 : (j + 1) * 32, 0:LANES], g[j * 32 : (j + 1) * 32, LANES:256]
        hr[j] = a * c - b * s
        hi[j] = a * s + b * c
    g0, g8 = g[0:32, 0:LANES], g[0:32, LANES:256]
    out = {}
    for b in range(5):
        even = g0 + g8 if b % 2 == 0 else g0 - g8
        odd = jnp.zeros_like(even)
        s_even, s_odd = jnp.zeros_like(even), jnp.zeros_like(even)
        for j in range(1, 8):
            c, s = np.cos(2 * np.pi * b * j / 16), np.sin(2 * np.pi * b * j / 16)
            tc = hr[j] * float(c) if abs(c) > 1e-9 else None
            ts = hi[j] * float(s) if abs(s) > 1e-9 else None
            if j % 2 == 0:
                even = even + tc if tc is not None else even
                s_even = s_even + ts if ts is not None else s_even
            else:
                odd = odd + tc if tc is not None else odd
                s_odd = s_odd + ts if ts is not None else s_odd
        cos_b, sin_b = even + odd, s_even + s_odd
        cos_c, sin_c = even - odd, s_odd - s_even
        out[b] = cos_b - sin_b
        out[(NB - b) % NB] = cos_b + sin_b
        out[8 - b] = cos_c - sin_c
        out[8 + b] = cos_c + sin_c
    lane = lax.broadcasted_iota(jnp.int32, (ROWS, LANES), 1)
    tail = corner_ref[0:4, :]
    from_right = lax.broadcasted_iota(jnp.int32, (3, LANES), 1) % 4 < 2
    for b in range(NB):
        after, before = (b + 1) % NB, (b - 1) % NB
        out_ref[b * SLOT : b * SLOT + 32, :] = out[b]
        border = jnp.where(lane < 2, out[after], out[before])
        edge = jnp.where(
            from_right,
            lines[after * SLOT + 33 : after * SLOT + 36, :],
            lines[before * SLOT + 33 : before * SLOT + 36, :],
        )
        out_ref[b * SLOT + 32 : (b + 1) * SLOT, :] = jnp.concatenate([pack(border), edge, tail], axis=0)


def wide(main, side, n, low, high):
    if n is None:
        return jnp.zeros((high - low, 2 * LANES), F32)
    rows = slice(n * 48 + low, n * 48 + high)
    return jnp.concatenate([main[rows, :], side[rows, :]], axis=1)


def near(base, l):
    return base + l if 0 <= l < LAYERS else None


def star_kernel(p_ref, al_ref, lo_ref, hi_ref, phi_ref, par, qm, qs, pm, ps):
    from_right = lax.broadcasted_iota(jnp.int32, (1, LANES), 1) % 4 < 2
    by = lax.axis_index("by")
    left, right = (by + NB - 1) % NB, (by + 1) % NB
    corner_lo = unpack(phi_ref[32 // 3, 33 + 32 % 3 : 34 + 32 % 3, :])
    corner_hi = unpack(jnp.where(from_right, phi_ref[right, 36:37, :], phi_ref[left, 36:37, :]))
    for n in range(32):
        ref, m = (p_ref, n) if n < 24 else (al_ref, n - 24)
        pm[n * 48 + 8 : n * 48 + 40, :] = ref[m * ROWS : (m + 1) * ROWS, :]
        ps[n * 48 + 8 : n * 48 + 40, :] = unpack(phi_ref[n // 3, 33 + n % 3 : 34 + n % 3, :])
    for row, value, corner in (
        (6, lo_ref[64:96, :], corner_lo),
        (7, lo_ref[96:128, :], corner_lo),
        (40, hi_ref[0:32, :], corner_hi),
        (41, hi_ref[32:64, :], corner_hi),
    ):
        pm[pl.ds(row, 32, stride=48), :] = value
        ps[pl.ds(row, 32, stride=48), :] = corner
    for l in range(LAYERS):
        p = [wide(pm, ps, c * LAYERS + l, 7, 41) for c in range(3)]
        total = p[0] * p[0] + p[1] * p[1] + p[2] * p[2]
        alpha2 = 2.0 * wide(pm, ps, 24 + l, 7, 41)
        e = coefficient(par, 3, l, 2 * LANES)
        landau = [coefficient(par, k, l, 2 * LANES) for k in range(3)]
        for c in range(3):
            n = c * LAYERS + l
            drive = drive_of(p[c], alpha2, total, *landau)
            lap = (
                wide(pm, ps, n, 8, 42) + wide(pm, ps, n, 6, 40) + shift(p[c], -1) + shift(p[c], 1)
                + wide(pm, ps, near(c * LAYERS, l + 1), 7, 41)
                + wide(pm, ps, near(c * LAYERS, l - 1), 7, 41)
                - 6.0 * p[c]
            )
            value = p[c] - DT * drive + e * lap
            qm[n * 48 + 7 : n * 48 + 41, :] = value[:, 0:LANES]
            qs[n * 48 + 7 : n * 48 + 41, :] = value[:, LANES : 2 * LANES]


def update_kernel(al_ref, qm, qs, phi_ref, far_ref, par, out_ref, field_ref, fm, fs, rm, rs, ht):
    for src in range(NB):
        ht[src * 32 : (src + 1) * 32, :] = unpack(phi_ref[src * SLOT + 32 : src * SLOT + 33, :])
    for f in range(2):
        for l in range(LAYERS):
            for xl in range(2):
                r = f * 16 + xl * 8 + l
                row = (f * LAYERS + l) * 48 + 8 + SHIFT + xl * NB
                fm[row : row + NB, :] = phi_ref[pl.ds(r, NB, stride=SLOT), :]
                fs[row : row + NB, :] = ht[pl.ds(r, NB, stride=32), :]
    for k in range(4):
        side = unpack(far_ref[k * SLOT + 32 : k * SLOT + 33, :])
        for f in range(2):
            rows = pl.ds(f * LAYERS * 48 + 6 + k, LAYERS, stride=48)
            fm[rows, :] = far_ref[k * SLOT + f * 16 + 8 : k * SLOT + f * 16 + 16, :]
            fs[rows, :] = side[f * 16 + 8 : f * 16 + 16]
    for l in range(LAYERS):
        phi = wide(fm, fs, l, 7, 41)
        slope = (
            wide(fm, fs, l, 8, 42) - wide(fm, fs, l, 6, 40),
            shift(phi, -1) - shift(phi, 1),
            wide(fm, fs, near(0, l + 1), 7, 41) - wide(fm, fs, near(0, l - 1), 7, 41),
        )
        for c in range(3):
            rows = slice((c * LAYERS + l) * 48 + 7, (c * LAYERS + l) * 48 + 41)
            rm[rows, :] = qm[rows, :] - (0.5 * DT) * slope[c][:, 0:LANES]
            rs[rows, :] = qs[rows, :] - (0.5 * DT) * slope[c][:, LANES : 2 * LANES]

    def at(ref, base, l, low, high):
        if 0 <= l < LAYERS:
            return ref[(base + l) * 48 + low : (base + l) * 48 + high, :]
        return jnp.zeros((high - low, LANES), F32)

    for l in range(LAYERS):
        p = [at(rm, c * LAYERS, l, 8, 40) for c in range(3)]
        total = p[0] * p[0] + p[1] * p[1] + p[2] * p[2]
        alpha2 = 2.0 * al_ref[l * ROWS : (l + 1) * ROWS, :]
        e = coefficient(par, 3, l)
        landau = [coefficient(par, k, l) for k in range(3)]
        phi = wide(fm, fs, LAYERS + l, 8, 40)
        field = (
            -0.5 * (at(fm, LAYERS, l, 9, 41) - at(fm, LAYERS, l, 7, 39)),
            -0.5 * (shift(phi, -1) - shift(phi, 1))[:, 0:LANES],
            -0.5 * (at(fm, LAYERS, l + 1, 8, 40) - at(fm, LAYERS, l - 1, 8, 40)),
        )
        for c in range(3):
            n = c * LAYERS + l
            drive = drive_of(p[c], alpha2, total, *landau)
            both = wide(rm, rs, n, 8, 40)
            lap = (
                at(rm, c * LAYERS, l, 9, 41) + at(rm, c * LAYERS, l, 7, 39)
                + (shift(both, -1) + shift(both, 1))[:, 0:LANES]
                + at(rm, c * LAYERS, l + 1, 8, 40) + at(rm, c * LAYERS, l - 1, 8, 40)
                - 6.0 * p[c]
            )
            out_ref[n * ROWS : (n + 1) * ROWS, :] = p[c] - DT * (drive - field[c]) + e * lap
            field_ref[n * ROWS : (n + 1) * ROWS, :] = field[c]


VMEM = pl.BlockSpec(memory_space=pltpu.VMEM)
HBM = pl.BlockSpec(memory_space=pltpu.HBM)


def call(kernel, shapes, specs, scratch, name):
    many = isinstance(shapes, list)
    return pl.pallas_call(
        kernel,
        out_shape=[jax.ShapeDtypeStruct(s, F32) for s in shapes]
        if many
        else jax.ShapeDtypeStruct(shapes, F32),
        in_specs=specs,
        out_specs=[VMEM] * len(shapes) if many else VMEM,
        scratch_shapes=[s if not isinstance(s, tuple) else pltpu.VMEM(s, F32) for s in scratch],
        compiler_params=PARAMS,
        name=name,
    )


def shards(tabs, polarization, alpha_field, landau, stiffness, permittivity, interfaces):
    count = lax.axis_size("bx")
    devices = count * NB
    ahead = [(i, (i + 1) % count) for i in range(count)]
    behind = [(i, (i - 1) % count) for i in range(count)]
    cells = polarization.reshape(24 * ROWS, LANES)
    alpha = alpha_field.reshape(LAYERS * ROWS, LANES)
    par = jnp.concatenate(
        [(landau * np.array([[4.0], [2.0], [6.0]], np.float32)).reshape(24), DT * stiffness, permittivity, interfaces]
    )
    par = jnp.broadcast_to(par[:, None], (par.shape[0], 2 * LANES))
    last, first = call(
        border_kernel, [(128, LANES), (64, LANES)], [HBM] * 2,
        [(2, 32, 8, LANES), pltpu.SemaphoreType.DMA((4,))], "border",
    )(polarization.reshape(24, ROWS, LANES), alpha_field)
    low = lax.ppermute(last, "bx", ahead)
    high = lax.ppermute(first, "bx", behind)
    sent = call(
        charge_kernel, (NB * SLOT, LANES), [VMEM] * 4,
        [(32 * 40, LANES), (24 * 40, LANES), (NB * 32, LANES), (48, LANES)], "charge",
    )(cells, alpha, low, par)
    lines = lax.all_to_all(sent.reshape(NB, SLOT, LANES), "by", 0, 0, tiled=True).reshape(NB * SLOT, LANES)
    modes, corner = call(
        y_forward_kernel, [(devices, LANES), (8, LANES)], [VMEM] * 7, [(256, 256)] * 2, "y_forward"
    )(lines, *tabs["fwd"], *tabs["fwd0"], tabs["tw"], high)
    modes = lax.all_to_all(modes.reshape(devices, 1, LANES), ("bx", "by"), 0, 0, tiled=True)
    modes = call(
        x_kernel, (devices, LANES), [VMEM] * 7,
        [(2 * devices, LANES), (2 * devices, LANES)], "x_solve",
    )(
        modes.reshape(devices, LANES), *tabs["x"], *tabs["xt"], tabs["lam"], par
    )
    modes = lax.all_to_all(modes.reshape(devices, 1, LANES), ("bx", "by"), 0, 0, tiled=True)
    sent = call(
        y_inverse_kernel, (NB * SLOT, LANES), [VMEM] * 8, [(256, 256)], "y_inverse"
    )(modes.reshape(devices, LANES), *tabs["inv"], *tabs["inv0"], tabs["tw"], lines, corner)
    phi = lax.all_to_all(sent.reshape(NB, SLOT, LANES), "by", 0, 0, tiled=True)
    far = lax.ppermute(phi[NB - 4 :].reshape(4 * SLOT, LANES), "bx", ahead)
    star = call(
        star_kernel, [(24 * 48, LANES)] * 2, [VMEM] * 6,
        [(32 * 48, LANES)] * 2, "star",
    )(cells, alpha, low, high, phi, par)
    polar, field = call(
        update_kernel, [(24 * ROWS, LANES)] * 2, [VMEM] * 6,
        [(16 * 48, LANES)] * 2 + [(24 * 48, LANES)] * 2 + [(NB * 32, LANES)], "update",
    )(alpha, *star, phi.reshape(NB * SLOT, LANES), far, par)
    return polar.reshape(polarization.shape), field.reshape(polarization.shape)


def solution(mesh):
    fwd, fwd0, inv, inv0, tw = tables_y()
    table, lam = tables_x(mesh.shape["bx"] * ROWS, -SHIFT)
    back, _ = tables_x(mesh.shape["bx"] * ROWS, SHIFT)
    tabs = {
        "fwd": split_table(fwd), "fwd0": split_table(fwd0),
        "inv": split_table(inv), "inv0": split_table(inv0),
        "tw": tw, "x": split_table(table), "xt": split_table(back.T), "lam": lam,
    }
    return jax.shard_map(
        functools.partial(shards, tabs),
        mesh=mesh,
        in_specs=(P(None, None, "bx", "by"), P(None, "bx", "by"), P(), P(), P(), P()),
        out_specs=(P(None, None, "bx", "by"), P(None, None, "bx", "by")),
        check_vma=False,
    )
```

```python
import functools

import jax
import jax.numpy as jnp
import ml_dtypes
import numpy as np
from jax import lax
from jax.experimental import pallas as pl
from jax.experimental.pallas import tpu as pltpu
from jax.sharding import PartitionSpec as P

DT = 0.05
NB = 16
LANES = 128
ROWS = 32
LAYERS = 8
SLOT = 40
SHIFT = 2
F32 = jnp.float32
BF16 = jnp.bfloat16
MICROSECONDS = {
    "border": 0.8, "stage": 1.8, "charge": 0.5, "load_y": 0.5,   "y_forward": 0.9, "x_solve": 1.5, "y_inverse": 0.8, "star": 1.3, "inner": 1.8, "update": 1.0
}


def split_table(table):
    high = table.astype(ml_dtypes.bfloat16)
    low = (table - high.astype(np.float64)).astype(ml_dtypes.bfloat16)
    return high, low


def tables_y():
    n = NB * LANES
    t = np.arange(LANES)
    k = np.arange(LANES)
    ang = 2 * np.pi * np.outer(k, t) / LANES
    c, s = np.cos(ang), np.sin(ang)
    fwd = np.block([[c, s], [-s, c]])
    inv = np.block([[c.T, -s.T], [s.T, c.T]]) * (2.0 / n)
    fwd0 = np.zeros((256, 256))
    inv0 = np.zeros((256, 256))
    for i in range(LANES):
        m = i if i <= 64 else i - 64
        wave = np.cos(2 * np.pi * m * t / LANES) if i <= 64 else np.sin(2 * np.pi * m * t / LANES)
        fwd0[i, :LANES] = wave
        inv0[:LANES, i] = wave * ((1.0 if i in (0, 64) else 2.0) / n)
    for i in range(64):
        th = 2 * np.pi * (8 + 16 * i) * t / n
        fwd0[128 + i, LANES:] = np.cos(th)
        fwd0[192 + i, LANES:] = -np.sin(th)
        inv0[LANES:, 128 + i] = np.cos(th) * (2.0 / n)
        inv0[LANES:, 192 + i] = -np.sin(th) * (2.0 / n)
    tw = np.zeros((16, LANES), np.float32)
    for j in range(8):
        tw[j] = np.cos(2 * np.pi * j * t / n)
        tw[8 + j] = np.sin(2 * np.pi * j * t / n)
    return fwd, fwd0, inv, inv0, tw


def tables_x(nx, offset):
    half = nx // 2
    pos = np.array(
        [
            bx * ROWS + xl * NB + by + offset
            for xl in range(2)
            for bx in range(half // ROWS)
            for by in range(NB)
        ]
    )
    even, odd = list(range(0, half + 1, 2)), list(range(1, half, 2))
    kinds = [(k, 0) for k in even] + [(k, 1) for k in even[1:-1]] + [(k, 0) for k in odd] + [(k, 1) for k in odd]
    scale = np.sqrt(2.0 / nx)
    rows = []
    for k, kind in kinds:
        wave = (np.sin if kind else np.cos)(2 * np.pi * (k * pos % nx) / nx)
        rows.append(wave * (np.sqrt(1.0 / nx) if k in (0, half) else scale))
    freq = np.array([k for k, _ in kinds])
    lam = np.stack([4 * np.sin(np.pi * freq / nx) ** 2, np.sin(2 * np.pi * freq / nx) ** 2])
    return np.stack(rows), lam.reshape(-1, LANES).astype(np.float32)


def split(value):
    high = value.astype(BF16)
    return high, (value - high.astype(F32)).astype(BF16)


def dot(a, b):
    return lax.dot_general(a, b, (((1,), (0,)), ((), ())), preferred_element_type=F32)


def dot_t(a, b):
    return lax.dot_general(a, b, (((1,), (1,)), ((), ())), preferred_element_type=F32)


def shift(value, by):
    n = value.shape[1]
    return pltpu.roll(value, by % n, axis=1)


def pack(tile):
    lane = lax.broadcasted_iota(jnp.int32, tile.shape, 1)
    edge = jnp.where((lane < 2) | (lane >= 126), tile, 0.0)
    return jnp.sum(pltpu.roll(edge, 0, axis=1, stride=4, stride_axis=0), axis=0, keepdims=True)


def unpack(row):
    value = jnp.broadcast_to(row, (8, LANES))
    index = lax.broadcasted_iota(jnp.int32, (8, LANES), 0)
    for bit in (1, 2, 4):
        value = jnp.where(index // bit % 2 == 1, pltpu.roll(value, LANES - 4 * bit, axis=1), value)
    return jnp.concatenate(
        [value] + [pltpu.roll(value, LANES - 32 * t, axis=1) for t in range(1, 4)], axis=0
    )


def drive_of(value, alpha2, total, quartic, mixed, sextic):
    sq = value * value
    return value * (alpha2 + quartic * sq + mixed * (total - sq) + sextic * (sq * sq))


def coefficient(par, kind, l, width=LANES):
    row = par[kind * LAYERS + l : kind * LAYERS + l + 1, 0:width]
    return row if kind > 3 else (4.0, 2.0, 6.0, DT)[kind] * row


def border_kernel(p_ref, al_ref, last_ref, buf, sems):
    copies = [
        pltpu.make_async_copy(src.at[:, pl.ds(ROWS - 8, 8), :], buf.at[cells], sems.at[k])
        for k, (src, cells) in enumerate(((p_ref, pl.ds(0, 24)), (al_ref, pl.ds(24, 8))))
    ]
    for copy in copies:
        copy.start()
    for copy in copies:
        copy.wait()
    for n in range(32):
        for r in range(4):
            last_ref[r * 32 + n : r * 32 + n + 1, :] = buf[n, 4 + r : 5 + r, :]


def load_kernel(table, hi_ref, after, table_ref, corner_ref, sem):
    copy = pltpu.make_async_copy(table, table_ref, sem.at[0])
    copy.start()
    corner_ref[...] = jnp.concatenate([pack(hi_ref[0:32, :]), jnp.zeros((7, LANES), F32)], axis=0)
    copy.wait()


def rows_of(ref, c, l, low, high):
    if 0 <= l < LAYERS:
        n = c * LAYERS + l
        return ref[n * 40 + low : n * 40 + high, :]
    return jnp.zeros((high - low, LANES), F32)


def charges(px, nx, par, low, high, store):
    at = rows_of
    first, last = low - 1, high + 1
    for l in range(LAYERS):
        p = [at(px, c, l, first, last) for c in range(3)]
        total = p[0] * p[0] + p[1] * p[1] + p[2] * p[2]
        alpha2 = 2.0 * at(px, 3, l, first, last)
        e = coefficient(par, 3, l)
        landau = [coefficient(par, k, l) for k in range(3)]
        for c in range(3):
            drive = drive_of(p[c], alpha2, total, *landau)
            lap = (
                at(px, c, l, first + 1, last + 1) + at(px, c, l, first - 1, last - 1)
                + at(px, c, l + 1, first, last) + at(px, c, l - 1, first, last)
                - 6.0 * p[c]
            )
            n = c * LAYERS + l
            nx[n * 40 + first : n * 40 + last, :] = p[c] - DT * drive + e * lap
    lane = lax.broadcasted_iota(jnp.int32, (high - low, LANES), 1)
    for l in range(LAYERS):
        e = coefficient(par, 3, l)
        dx = -0.5 * (at(px, 0, l, low + 1, high + 1) - at(px, 0, l, low - 1, high - 1))
        above, below = at(px, 2, l + 1, low, high), at(px, 2, l - 1, low, high)
        p1, n1 = at(px, 1, l, low, high), at(nx, 1, l, low, high)
        fwd, bwd = shift(p1, -1), shift(p1, 1)
        one = dx - 0.5 * (above - below) - 0.5 * (fwd - bwd)
        wrap_one = jnp.where(lane == LANES - 1, -0.5 * fwd, jnp.where(lane == 0, 0.5 * bwd, 0.0))
        e_up = coefficient(par, 3, l + 1) if l + 1 < LAYERS else 0.0
        e_dn = coefficient(par, 3, l - 1) if l > 0 else 0.0
        ue = e * dx - 0.5 * (e_up * above - e_dn * below)
        un = -0.5 * (at(nx, 0, l, low + 1, high + 1) - at(nx, 0, l, low - 1, high - 1)) - 0.5 * (
            at(nx, 2, l + 1, low, high) - at(nx, 2, l - 1, low, high)
        )
        a = shift(ue - 0.5 * n1, -1)
        b = shift(ue + 0.5 * n1, 1)
        h = (0.5 * e) * p1
        c2, d2 = shift(h, -2), shift(h, 2)
        two = un + a + b - c2 + d2
        wrap_two = (
            jnp.where(lane == LANES - 1, a, 0.0)
            + jnp.where(lane == 0, b, 0.0)
            + jnp.where(lane >= LANES - 2, -c2, 0.0)
            + jnp.where(lane < 2, d2, 0.0)
        )
        store(0, l, one - wrap_one, wrap_one)
        store(1, l, two - wrap_two, wrap_two)


def stage_kernel(p_ref, al_ref, par, after, out_ref, head_ref, first_ref, px, nx, ws, eb):
    for n in range(32):
        ref, m = (p_ref, n) if n < 24 else (al_ref, n - 24)
        px[n * 40 + 8 : n * 40 + 40, :] = ref[m * ROWS : (m + 1) * ROWS, :]
        head_ref[n * 8 : (n + 1) * 8, :] = ref[m * ROWS : m * ROWS + 8, :]
        eb[n : n + 1, :] = pack(ref[m * ROWS : (m + 1) * ROWS, :])
    eb[32:48, :] = jnp.zeros((16, LANES), F32)
    for r in range(2):
        first_ref[r * 32 : (r + 1) * 32, :] = px[pl.ds(8 + r, 32, stride=40), :]

    def store(f, l, main, wrap):
        r = f * 16 + l
        out_ref[pl.ds(4 * SLOT + r, 12, stride=SLOT), :] = main[0:12]
        ws[pl.ds(4 * 32 + r, 12, stride=32), :] = wrap[0:12]
        out_ref[pl.ds(r + 8, NB, stride=SLOT), :] = main[12:28]
        ws[pl.ds(r + 8, NB, stride=32), :] = wrap[12:28]
        for b in range(4):
            ws[b * 32 + r : b * 32 + r + 1, :] = jnp.zeros((1, LANES), F32)
            out_ref[b * SLOT + r : b * SLOT + r + 1, :] = jnp.zeros((1, LANES), F32)

    charges(px, nx, par, 10, 38, store)
    blank = jnp.zeros((4, LANES), F32)
    for b in range(NB):
        out_ref[b * SLOT + 32 : (b + 1) * SLOT, :] = jnp.concatenate(
            [pack(ws[b * 32 : (b + 1) * 32, :]), eb[3 * b : 3 * b + 3, :], blank], axis=0
        )


def charge_kernel(part_ref, head_ref, lo_ref, par, out_ref, px, nx, ws):
    out_ref[...] = part_ref[...]
    for n in range(32):
        px[n * 40 + 8 : n * 40 + 16, :] = head_ref[n * 8 : (n + 1) * 8, :]
    for r in range(4):
        px[pl.ds(4 + r, 32, stride=40), :] = lo_ref[r * 32 : (r + 1) * 32, :]
    ws[...] = jnp.zeros_like(ws)

    def store(f, l, main, wrap):
        r = f * 16 + l
        for b in range(4):
            out_ref[b * SLOT + r : b * SLOT + r + 1, :] = main[b : b + 1]
            ws[b * 32 + r : b * 32 + r + 1, :] = wrap[b : b + 1]

    charges(px, nx, par, 6, 10, store)
    for b in range(4):
        out_ref[b * SLOT + 32 : b * SLOT + 33, :] = part_ref[b * SLOT + 32 : b * SLOT + 33, :] + pack(
            ws[b * 32 : (b + 1) * 32, :]
        )
    at = (32 // 3) * SLOT + 33 + 32 % 3
    out_ref[at : at + 1, :] = pack(lo_ref[96:128, :])


def y_forward_kernel(in_ref, tab, tw, out_ref, d_ref, o_ref):
    fh, fl, f0h, f0l = (tab[k * 256 : (k + 1) * 256, :] for k in range(4))
    lane1 = lax.broadcasted_iota(jnp.int32, (1, LANES), 1)
    lane = lax.broadcasted_iota(jnp.int32, (ROWS, LANES), 1)
    g = []
    for b in range(NB):
        before = in_ref[((b - 1) % NB) * SLOT + 32 : ((b - 1) % NB) * SLOT + 33, :]
        after = in_ref[((b + 1) % NB) * SLOT + 32 : ((b + 1) % NB) * SLOT + 33, :]
        extra = unpack(jnp.where(lane1 % 4 < 2, before, after))
        g.append(
            in_ref[b * SLOT : b * SLOT + 32, :]
            + jnp.where((lane < 2) | (lane >= 126), extra, 0.0)
        )
    plus = {b: g[b] + g[NB - b] for b in range(1, 8)}
    minus = {b: g[b] - g[NB - b] for b in range(1, 8)}
    re, im = {}, {}
    for k in range(5):
        even = g[0] + g[8] if k % 2 == 0 else g[0] - g[8]
        odd = jnp.zeros_like(even)
        s_even, s_odd = jnp.zeros_like(even), jnp.zeros_like(even)
        for b in range(1, 8):
            c, s = np.cos(2 * np.pi * b * k / 16), np.sin(2 * np.pi * b * k / 16)
            tc = plus[b] * float(c) if abs(c) > 1e-9 else None
            ts = minus[b] * float(s) if abs(s) > 1e-9 else None
            if b % 2 == 0:
                even = even + tc if tc is not None else even
                s_even = s_even + ts if ts is not None else s_even
            else:
                odd = odd + tc if tc is not None else odd
                s_odd = s_odd + ts if ts is not None else s_odd
        re[k], re[8 - k] = even + odd, even - odd
        im[k], im[8 - k] = -(s_even + s_odd), s_even - s_odd
    d_ref[0:32, 0:LANES] = re[0]
    d_ref[0:32, LANES:256] = re[8]
    for j in range(1, 8):
        c, s = tw[j : j + 1, :], tw[8 + j : 9 + j, :]
        d_ref[j * 32 : (j + 1) * 32, 0:LANES] = re[j] * c + im[j] * s
        d_ref[j * 32 : (j + 1) * 32, LANES:256] = im[j] * c - re[j] * s
    dh, dl = split(d_ref[...])
    o_ref[...] = dot_t(fh, dh) + dot_t(fh, dl) + dot_t(fl, dh)
    zero = dot_t(f0h, dh[0:128]) + dot_t(f0h, dl[0:128]) + dot_t(f0l, dh[0:128])
    wide = lax.broadcasted_iota(jnp.int32, (256, LANES), 1)
    o_ref[:, 0:LANES] = jnp.where(wide < 32, zero, o_ref[:, 0:LANES])
    lane64 = lax.broadcasted_iota(jnp.int32, (64, LANES), 1)
    for j in range(8):
        t, at = j // 4, j % 4
        value = None
        for q in range(4):
            piece = o_ref[q * 64 : (q + 1) * 64, t * LANES : (t + 1) * LANES]
            if q != at:
                piece = shift(piece, (q - at) * 32)
            value = piece if value is None else jnp.where(lane64 // 32 == q, piece, value)
        out_ref[j * 64 : (j + 1) * 64, :] = value


def x_kernel(in_ref, th, tl, lam, par, out_ref, zs, ys):
    n = in_ref.shape[0]
    half = n // 2
    top, low = in_ref[0:half, :], in_ref[half:n, :]
    for part, value in enumerate((top + low, top - low)):
        high, rest = split(value)
        both = jnp.concatenate([high, rest], axis=1)
        for chunk in range(n // 256):
            r0 = part * n + chunk * 256
            acc = []
            for xl in range(2):
                cols = slice(xl * half, (xl + 1) * half)
                wide = dot(th[r0 : r0 + 256, cols], both)
                acc.append(
                    wide[:, 0:LANES] + wide[:, LANES:256] + dot(tl[r0 : r0 + 256, cols], high)
                )
            turned = jnp.transpose(acc[0] + shift(acc[1], -8))
            zs[r0 : r0 + LANES, :] = turned[:, 0:LANES]
            zs[r0 + LANES : r0 + 256, :] = turned[:, LANES:256]
    dev = lax.axis_index("bx") * NB + lax.axis_index("by")
    j = dev // 64
    q = lax.broadcasted_iota(jnp.int32, (8, 1), 0) // 2
    s = q * 64 + dev % 64
    ky_j = j + 16 * (s % 128)
    ky_0 = jnp.where(s < 128, 16 * jnp.where(s <= 64, s, s - 64), 8 + 16 * (s % 64))
    ky = jnp.where(j == 0, ky_0, ky_j)
    full = NB * LANES
    ky = jnp.minimum(ky, full - ky).astype(F32)
    ky = jnp.broadcast_to(ky, (8, LANES))
    sin_half = jnp.sin(ky * (np.pi / full))
    lam_y = 4.0 * sin_half * sin_half
    sin_y = jnp.sin(jnp.minimum(ky, full // 2 - ky) * (2.0 * np.pi / full))
    slope_y = sin_y * sin_y
    second = lax.broadcasted_iota(jnp.int32, (8, LANES), 0) % 2 == 1
    eps = [coefficient(par, 4, l) for l in range(LAYERS)]
    iface = [coefficient(par, 5, l) for l in range(LAYERS + 1)]
    for chunk in range(2 * n // LANES):
        lateral = lam_y + lam[16 + chunk : 17 + chunk, :]
        slope = slope_y + lam[16 + 2 * n // LANES + chunk : 17 + 2 * n // LANES + chunk, :]
        inverse, ratio = [], []
        for l in range(LAYERS):
            pivot = eps[l] * lateral + (iface[l] + iface[l + 1])
            if l > 0:
                pivot = pivot - iface[l] * ratio[-1]
            inverse.append(1.0 / pivot)
            ratio.append(iface[l + 1] * inverse[-1])

        def solve(source):
            prime = []
            for l in range(LAYERS):
                value = source[l] + iface[l] * prime[-1] if l > 0 else source[l]
                prime.append(value * inverse[l])
            for l in range(LAYERS - 2, -1, -1):
                prime[l] = prime[l] + ratio[l] * prime[l + 1]
            return prime

        phi = solve([zs[pl.ds(chunk * LANES + l, 8, stride=16), :] for l in range(LAYERS)])
        first = [jnp.where(second, pltpu.roll(v, 1, axis=0), 0.0) for v in phi]
        zero = jnp.zeros_like(first[0])

        def dz(v):
            return [
                0.5 * ((v[l + 1] if l + 1 < LAYERS else zero) - (v[l - 1] if l > 0 else zero))
                for l in range(LAYERS)
            ]

        twice = dz(dz(first))
        more = solve([DT * (twice[l] - slope * first[l]) for l in range(LAYERS)])
        for l in range(LAYERS):
            value = phi[l] + more[l]
            ys[pl.ds(chunk * LANES + l, 8, stride=16), :] = value
            ys[pl.ds(chunk * LANES + 8 + l, 8, stride=16), :] = value
    odd_row = lax.broadcasted_iota(jnp.int32, (LANES, half), 0) // 8 % 2 == 1
    pair = []
    for part in range(2):
        high, rest = split(
            jnp.concatenate([ys[r : r + LANES, :] for r in range(part * n, (part + 1) * n, LANES)], axis=1)
        )
        rows = slice(part * n, (part + 1) * n)
        both = dot(jnp.concatenate([high, rest], axis=0), th[rows, :])
        both = both[0:LANES] + both[LANES:256] + dot(high, tl[rows, :])
        pair.append(jnp.where(odd_row, both[:, half:n], both[:, 0:half]))
    out_ref[0:half, :] = jnp.transpose(pair[0] + pair[1])
    out_ref[half:n, :] = jnp.transpose(pair[0] - pair[1])


def y_inverse_kernel(in_ref, tab, tw, lines, corner_ref, out_ref, o_ref):
    gh, gl, g0h, g0l = (tab[k * 256 : (k + 1) * 256, :] for k in range(4))
    lane64 = lax.broadcasted_iota(jnp.int32, (64, LANES), 1)
    for t in range(2):
        for q in range(4):
            value = None
            for at in range(4):
                j = t * 4 + at
                piece = in_ref[j * 64 : (j + 1) * 64, :]
                if q != at:
                    piece = shift(piece, (at - q) * 32)
                value = piece if value is None else jnp.where(lane64 // 32 == at, piece, value)
            o_ref[q * 64 : (q + 1) * 64, t * LANES : (t + 1) * LANES] = value
    oh, ol = split(o_ref[...])
    o_ref[...] = dot(gh, oh) + dot(gh, ol) + dot(gl, oh)
    zero = (
        dot(g0h, oh[:, 0:LANES]) + dot(g0h, ol[:, 0:LANES]) + dot(g0l, oh[:, 0:LANES])
    )
    wide = lax.broadcasted_iota(jnp.int32, (256, LANES), 1)
    o_ref[:, 0:LANES] = jnp.where(wide < 32, zero, o_ref[:, 0:LANES])
    g = jnp.transpose(o_ref[...])
    hr, hi = {}, {}
    for j in range(1, 8):
        c, s = tw[j : j + 1, :], tw[8 + j : 9 + j, :]
        a, b = g[j * 32 : (j + 1) * 32, 0:LANES], g[j * 32 : (j + 1) * 32, LANES:256]
        hr[j] = a * c - b * s
        hi[j] = a * s + b * c
    g0, g8 = g[0:32, 0:LANES], g[0:32, LANES:256]
    out = {}
    for b in range(5):
        even = g0 + g8 if b % 2 == 0 else g0 - g8
        odd = jnp.zeros_like(even)
        s_even, s_odd = jnp.zeros_like(even), jnp.zeros_like(even)
        for j in range(1, 8):
            c, s = np.cos(2 * np.pi * b * j / 16), np.sin(2 * np.pi * b * j / 16)
            tc = hr[j] * float(c) if abs(c) > 1e-9 else None
            ts = hi[j] * float(s) if abs(s) > 1e-9 else None
            if j % 2 == 0:
                even = even + tc if tc is not None else even
                s_even = s_even + ts if ts is not None else s_even
            else:
                odd = odd + tc if tc is not None else odd
                s_odd = s_odd + ts if ts is not None else s_odd
        cos_b, sin_b = even + odd, s_even + s_odd
        cos_c, sin_c = even - odd, s_odd - s_even
        out[b] = cos_b - sin_b
        out[(NB - b) % NB] = cos_b + sin_b
        out[8 - b] = cos_c - sin_c
        out[8 + b] = cos_c + sin_c
    lane = lax.broadcasted_iota(jnp.int32, (ROWS, LANES), 1)
    tail = corner_ref[0:4, :]
    from_right = lax.broadcasted_iota(jnp.int32, (3, LANES), 1) % 4 < 2
    for b in range(NB):
        after, before = (b + 1) % NB, (b - 1) % NB
        out_ref[b * SLOT : b * SLOT + 32, :] = out[b]
        border = jnp.where(lane < 2, out[after], out[before])
        edge = jnp.where(
            from_right,
            lines[after * SLOT + 33 : after * SLOT + 36, :],
            lines[before * SLOT + 33 : before * SLOT + 36, :],
        )
        out_ref[b * SLOT + 32 : (b + 1) * SLOT, :] = jnp.concatenate([pack(border), edge, tail], axis=0)


def wide(main, side, n, low, high):
    if n is None:
        return jnp.zeros((high - low, 2 * LANES), F32)
    rows = slice(n * 48 + low, n * 48 + high)
    return jnp.concatenate([main[rows, :], side[rows, :]], axis=1)


def edge_row(n):
    return n // 3 * SLOT + 33 + n % 3


def near(base, l):
    return base + l if 0 <= l < LAYERS else None


def layer_rows(ref, base, l, low, high):
    if 0 <= l < LAYERS:
        return ref[(base + l) * 48 + low : (base + l) * 48 + high, :]
    return jnp.zeros((high - low, LANES), F32)


def first_step(qm, qs, fm, fs, rm, rs, low, high):
    for l in range(LAYERS):
        phi = wide(fm, fs, l, low, high)
        slope = (
            wide(fm, fs, l, low + 1, high + 1) - wide(fm, fs, l, low - 1, high - 1),
            shift(phi, -1) - shift(phi, 1),
            wide(fm, fs, near(0, l + 1), low, high) - wide(fm, fs, near(0, l - 1), low, high),
        )
        for c in range(3):
            rows = slice((c * LAYERS + l) * 48 + low, (c * LAYERS + l) * 48 + high)
            rm[rows, :] = qm[rows, :] - (0.5 * DT) * slope[c][:, 0:LANES]
            rs[rows, :] = qs[rows, :] - (0.5 * DT) * slope[c][:, LANES : 2 * LANES]


def second_step(al_ref, fm, fs, rm, rs, par, low, high, store):
    at = layer_rows
    for l in range(LAYERS):
        p = [at(rm, c * LAYERS, l, low, high) for c in range(3)]
        total = p[0] * p[0] + p[1] * p[1] + p[2] * p[2]
        alpha2 = 2.0 * al_ref[l * ROWS + low - 8 : l * ROWS + high - 8, :]
        e = coefficient(par, 3, l)
        landau = [coefficient(par, k, l) for k in range(3)]
        phi = wide(fm, fs, LAYERS + l, low, high)
        field = (
            -0.5 * (at(fm, LAYERS, l, low + 1, high + 1) - at(fm, LAYERS, l, low - 1, high - 1)),
            -0.5 * (shift(phi, -1) - shift(phi, 1))[:, 0:LANES],
            -0.5 * (at(fm, LAYERS, l + 1, low, high) - at(fm, LAYERS, l - 1, low, high)),
        )
        for c in range(3):
            drive = drive_of(p[c], alpha2, total, *landau)
            both = wide(rm, rs, c * LAYERS + l, low, high)
            lap = (
                at(rm, c * LAYERS, l, low + 1, high + 1) + at(rm, c * LAYERS, l, low - 1, high - 1)
                + (shift(both, -1) + shift(both, 1))[:, 0:LANES]
                + at(rm, c * LAYERS, l + 1, low, high) + at(rm, c * LAYERS, l - 1, low, high)
                - 6.0 * p[c]
            )
            store(c * LAYERS + l, p[c] - DT * (drive - field[c]) + e * lap, field[c])


def star_kernel(p_ref, al_ref, lo_ref, hi_ref, phi_ref, par, qm, qs, pm, ps):
    from_right = lax.broadcasted_iota(jnp.int32, (1, LANES), 1) % 4 < 2
    by = lax.axis_index("by")
    left, right = (by + NB - 1) % NB, (by + 1) % NB
    corner_lo = unpack(phi_ref[edge_row(32) : edge_row(32) + 1, :])
    corner_hi = unpack(
        jnp.where(
            from_right, phi_ref[pl.ds(right * SLOT + 36, 1), :], phi_ref[pl.ds(left * SLOT + 36, 1), :]
        )
    )
    for n in range(32):
        ref, m = (p_ref, n) if n < 24 else (al_ref, n - 24)
        pm[n * 48 + 8 : n * 48 + 40, :] = ref[m * ROWS : (m + 1) * ROWS, :]
        ps[n * 48 + 8 : n * 48 + 40, :] = unpack(phi_ref[edge_row(n) : edge_row(n) + 1, :])
    for row, value, corner in (
        (6, lo_ref[64:96, :], corner_lo),
        (7, lo_ref[96:128, :], corner_lo),
        (40, hi_ref[0:32, :], corner_hi),
        (41, hi_ref[32:64, :], corner_hi),
    ):
        pm[pl.ds(row, 32, stride=48), :] = value
        ps[pl.ds(row, 32, stride=48), :] = corner
    for l in range(LAYERS):
        p = [wide(pm, ps, c * LAYERS + l, 7, 41) for c in range(3)]
        total = p[0] * p[0] + p[1] * p[1] + p[2] * p[2]
        alpha2 = 2.0 * wide(pm, ps, 24 + l, 7, 41)
        e = coefficient(par, 3, l, 2 * LANES)
        landau = [coefficient(par, k, l, 2 * LANES) for k in range(3)]
        for c in range(3):
            n = c * LAYERS + l
            drive = drive_of(p[c], alpha2, total, *landau)
            lap = (
                wide(pm, ps, n, 8, 42) + wide(pm, ps, n, 6, 40) + shift(p[c], -1) + shift(p[c], 1)
                + wide(pm, ps, near(c * LAYERS, l + 1), 7, 41)
                + wide(pm, ps, near(c * LAYERS, l - 1), 7, 41)
                - 6.0 * p[c]
            )
            value = p[c] - DT * drive + e * lap
            qm[n * 48 + 7 : n * 48 + 41, :] = value[:, 0:LANES]
            qs[n * 48 + 7 : n * 48 + 41, :] = value[:, LANES : 2 * LANES]


def inner_kernel(al_ref, qm, qs, phi_ref, par, out_ref, field_ref, fm, fs, rm, rs, ht):
    for src in range(NB):
        ht[src * 32 : (src + 1) * 32, :] = unpack(phi_ref[src * SLOT + 32 : src * SLOT + 33, :])
    for f in range(2):
        for l in range(LAYERS):
            for xl in range(2):
                r = f * 16 + xl * 8 + l
                row = (f * LAYERS + l) * 48 + 8 - SHIFT + xl * NB
                fm[row : row + NB, :] = phi_ref[pl.ds(r, NB, stride=SLOT), :]
                fs[row : row + NB, :] = ht[pl.ds(r, NB, stride=32), :]
    first_step(qm, qs, fm, fs, rm, rs, 7, 33)

    def store(n, value, field):
        out_ref[n, 0:24, :] = value
        field_ref[n, 0:24, :] = field

    second_step(al_ref, fm, fs, rm, rs, par, 8, 32, store)


def update_kernel(
    al_ref, qm, qs, gm, gs, far_ref, par, out_in, field_in, out_ref, field_ref, fm, fs, rm, rs, to, tf, sems
):
    for n in range(2 * LAYERS):
        fm[n * 48 + 30 : n * 48 + 38, :] = gm[n * 48 + 30 : n * 48 + 38, :]
        fs[n * 48 + 30 : n * 48 + 38, :] = gs[n * 48 + 30 : n * 48 + 38, :]
    for k in range(4):
        side = unpack(far_ref[k * SLOT + 32 : k * SLOT + 33, :])
        for f in range(2):
            rows = pl.ds(f * LAYERS * 48 + 38 + k, LAYERS, stride=48)
            fm[rows, :] = far_ref[k * SLOT + f * 16 : k * SLOT + f * 16 + 8, :]
            fs[rows, :] = side[f * 16 : f * 16 + 8]
    first_step(qm, qs, fm, fs, rm, rs, 31, 41)

    def store(n, value, field):
        to[n] = value
        tf[n] = field

    second_step(al_ref, fm, fs, rm, rs, par, 32, 40, store)
    copies = [
        pltpu.make_async_copy(src, dst.at[:, pl.ds(24, 8), :], sems.at[k])
        for k, (src, dst) in enumerate(((to, out_ref), (tf, field_ref)))
    ]
    for copy in copies:
        copy.start()
    for copy in copies:
        copy.wait()


VMEM = pl.BlockSpec(memory_space=pltpu.VMEM)
ANY = pl.BlockSpec(memory_space=pl.ANY)


def call(kernel, shapes, specs, scratch, name, out=VMEM, aliases=None, dtype=None, mib=16):
    many = isinstance(shapes, list)
    return pl.pallas_call(
        kernel,
        out_shape=[jax.ShapeDtypeStruct(s, d) for s, d in zip(shapes, dtype or [F32] * len(shapes))]
        if many
        else jax.ShapeDtypeStruct(shapes, F32),
        in_specs=specs,
        out_specs=[out] * len(shapes) if many else out,
        input_output_aliases=aliases or {},
        scratch_shapes=[s if not isinstance(s, tuple) else pltpu.VMEM(s, F32) for s in scratch],
        compiler_params=pltpu.CompilerParams(vmem_limit_bytes=int(mib * 1024 * 1024)),
        cost_estimate=pl.CostEstimate(flops=0, transcendentals=0, bytes_accessed=int(3.5e6 * MICROSECONDS[name])),
        name=name,
    )


def shards(tabs, polarization, alpha_field, landau, stiffness, permittivity, interfaces):
    count = lax.axis_size("bx")
    devices = count * NB
    ahead = [(i, (i + 1) % count) for i in range(count)]
    behind = [(i, (i - 1) % count) for i in range(count)]
    cells = polarization.reshape(24 * ROWS, LANES)
    alpha = alpha_field.reshape(LAYERS * ROWS, LANES)
    par = jnp.concatenate([landau[0], landau[1], landau[2], stiffness, permittivity, interfaces])
    par = jnp.broadcast_to(par[:, None], (par.shape[0], 2 * LANES))
    last = call(
        border_kernel, (128, LANES), [ANY] * 2,
        [(32, 8, LANES), pltpu.SemaphoreType.DMA((2,))], "border", mib=53.8,
    )(polarization.reshape(24, ROWS, LANES), alpha_field)
    low = lax.ppermute(last, "bx", ahead)
    part, head, first = call(
        stage_kernel, [(NB * SLOT, LANES), (256, LANES), (64, LANES)], [VMEM] * 3 + [ANY],
        [(32 * 40, LANES), (24 * 40, LANES), (NB * 32, LANES), (48, LANES)], "stage",
    )(cells, alpha, par, last)
    high = lax.ppermute(first, "bx", behind)
    sent = call(
        charge_kernel, (NB * SLOT, LANES), [VMEM] * 4,
        [(32 * 40, LANES), (24 * 40, LANES), (4 * 32, LANES)], "charge",
    )(part, head, low, par)
    fwd, corner = call(
        load_kernel, [tabs["fwd"].shape, (8, LANES)], [ANY, VMEM, ANY], [pltpu.SemaphoreType.DMA((1,))],
        "load_y", dtype=[BF16, F32],
    )(tabs["fwd"], high, sent)
    lines = lax.all_to_all(sent.reshape(NB, SLOT, LANES), "by", 0, 0, tiled=True).reshape(NB * SLOT, LANES)
    modes = call(
        y_forward_kernel, (devices, LANES), [VMEM] * 3, [(256, 256)] * 2, "y_forward"
    )(lines, fwd, tabs["small"])
    modes = lax.all_to_all(modes.reshape(devices, 1, LANES), ("bx", "by"), 0, 0, tiled=True)
    modes = call(
        x_kernel, (devices, LANES), [VMEM] * 5, [(2 * devices, LANES)] * 2, "x_solve"
    )(modes.reshape(devices, LANES), *tabs["x"], tabs["small"], par)
    modes = lax.all_to_all(modes.reshape(devices, 1, LANES), ("bx", "by"), 0, 0, tiled=True)
    sent = call(
        y_inverse_kernel, (NB * SLOT, LANES), [VMEM] * 5, [(256, 256)], "y_inverse"
    )(modes.reshape(devices, LANES), tabs["inv"], tabs["small"], lines, corner)
    phi = lax.all_to_all(sent.reshape(NB, SLOT, LANES), "by", 0, 0, tiled=True)
    far = lax.ppermute(phi[:4].reshape(4 * SLOT, LANES), "bx", behind)
    phi = phi.reshape(NB * SLOT, LANES)
    star = call(
        star_kernel, [(24 * 48, LANES)] * 2, [VMEM] * 6, [(32 * 48, LANES)] * 2, "star",
    )(cells, alpha, low, high, phi, par)
    polar, field, *grid = call(
        inner_kernel, [(24, ROWS, LANES)] * 2 + [(16 * 48, LANES)] * 2, [VMEM] * 5,
        [(24 * 48, LANES)] * 2 + [(NB * 32, LANES)], "inner",
    )(alpha, *star, phi, par)
    polar, field = call(
        update_kernel, [(24, ROWS, LANES)] * 2, [VMEM] * 7 + [ANY] * 2,
        [(16 * 48, LANES)] * 2 + [(24 * 48, LANES)] * 2 + [(24, 8, LANES)] * 2 + [pltpu.SemaphoreType.DMA((2,))],
        "update", out=ANY, aliases={7: 0, 8: 1},
    )(alpha, *star, *grid, far, par, polar, field)
    return polar.reshape(polarization.shape), field.reshape(polarization.shape)


def solution(mesh):
    fwd, fwd0, inv, inv0, tw = tables_y()
    table, lam = tables_x(mesh.shape["bx"] * ROWS, -SHIFT)
    tabs = {
        "fwd": np.concatenate([*split_table(fwd), *split_table(fwd0)], axis=0),
        "inv": np.concatenate([*split_table(inv), *split_table(inv0)], axis=0),
        "x": split_table(table),
        "small": np.concatenate([tw, lam], axis=0),
    }
    return jax.shard_map(
        functools.partial(shards, tabs),
        mesh=mesh,
        in_specs=(P(None, None, "bx", "by"), P(None, "bx", "by"), P(), P(), P(), P()),
        out_specs=(P(None, None, "bx", "by"), P(None, None, "bx", "by")),
        check_vma=False,
    )
```

```python
import functools

import jax
import jax.numpy as jnp
import ml_dtypes
import numpy as np
from jax import lax
from jax.experimental import pallas as pl
from jax.experimental.pallas import tpu as pltpu
from jax.sharding import PartitionSpec as P

DT = 0.05
NB = 16
LANES = 128
ROWS = 32
LAYERS = 8
SLOT = 40
SHIFT = 2
F32 = jnp.float32
BF16 = jnp.bfloat16
MICROSECONDS = {
    "border": 0.8, "stage": 1.8, "charge": 0.5,   "y_forward": 0.9, "x_solve": 1.5, "y_inverse": 0.8, "star": 1.3, "inner": 1.8, "update": 1.0
}


def split_table(table):
    high = table.astype(ml_dtypes.bfloat16)
    low = (table - high.astype(np.float64)).astype(ml_dtypes.bfloat16)
    return high, low


def tables_y():
    n = NB * LANES
    t = np.arange(LANES)
    k = np.arange(LANES)
    ang = 2 * np.pi * np.outer(k, t) / LANES
    c, s = np.cos(ang), np.sin(ang)
    fwd = np.block([[c, s], [-s, c]])
    inv = np.block([[c.T, -s.T], [s.T, c.T]]) * (2.0 / n)
    fwd0 = np.zeros((256, 256))
    inv0 = np.zeros((256, 256))
    for i in range(LANES):
        m = i if i <= 64 else i - 64
        wave = np.cos(2 * np.pi * m * t / LANES) if i <= 64 else np.sin(2 * np.pi * m * t / LANES)
        fwd0[i, :LANES] = wave
        inv0[:LANES, i] = wave * ((1.0 if i in (0, 64) else 2.0) / n)
    for i in range(64):
        th = 2 * np.pi * (8 + 16 * i) * t / n
        fwd0[128 + i, LANES:] = np.cos(th)
        fwd0[192 + i, LANES:] = -np.sin(th)
        inv0[LANES:, 128 + i] = np.cos(th) * (2.0 / n)
        inv0[LANES:, 192 + i] = -np.sin(th) * (2.0 / n)
    tw = np.zeros((16, LANES), np.float32)
    for j in range(8):
        tw[j] = np.cos(2 * np.pi * j * t / n)
        tw[8 + j] = np.sin(2 * np.pi * j * t / n)
    return fwd, fwd0, inv, inv0, tw


def tables_x(nx, offset):
    half = nx // 2
    pos = np.array(
        [
            bx * ROWS + xl * NB + by + offset
            for xl in range(2)
            for bx in range(half // ROWS)
            for by in range(NB)
        ]
    )
    even, odd = list(range(0, half + 1, 2)), list(range(1, half, 2))
    kinds = [(k, 0) for k in even] + [(k, 1) for k in even[1:-1]] + [(k, 0) for k in odd] + [(k, 1) for k in odd]
    scale = np.sqrt(2.0 / nx)
    rows = []
    for k, kind in kinds:
        wave = (np.sin if kind else np.cos)(2 * np.pi * (k * pos % nx) / nx)
        rows.append(wave * (np.sqrt(1.0 / nx) if k in (0, half) else scale))
    freq = np.array([k for k, _ in kinds])
    lam = np.stack([4 * np.sin(np.pi * freq / nx) ** 2, np.sin(2 * np.pi * freq / nx) ** 2])
    return np.stack(rows), lam.reshape(-1, LANES).astype(np.float32)


def split(value):
    high = value.astype(BF16)
    return high, (value - high.astype(F32)).astype(BF16)


def dot(a, b):
    return lax.dot_general(a, b, (((1,), (0,)), ((), ())), preferred_element_type=F32)


def dot_t(a, b):
    return lax.dot_general(a, b, (((1,), (1,)), ((), ())), preferred_element_type=F32)


def shift(value, by):
    n = value.shape[1]
    return pltpu.roll(value, by % n, axis=1)


def pack(tile):
    lane = lax.broadcasted_iota(jnp.int32, tile.shape, 1)
    edge = jnp.where((lane < 2) | (lane >= 126), tile, 0.0)
    return jnp.sum(pltpu.roll(edge, 0, axis=1, stride=4, stride_axis=0), axis=0, keepdims=True)


def unpack(row):
    value = jnp.broadcast_to(row, (8, LANES))
    index = lax.broadcasted_iota(jnp.int32, (8, LANES), 0)
    for bit in (1, 2, 4):
        value = jnp.where(index // bit % 2 == 1, pltpu.roll(value, LANES - 4 * bit, axis=1), value)
    return jnp.concatenate(
        [value] + [pltpu.roll(value, LANES - 32 * t, axis=1) for t in range(1, 4)], axis=0
    )


def drive_of(value, alpha2, total, quartic, mixed, sextic):
    sq = value * value
    return value * (alpha2 + quartic * sq + mixed * (total - sq) + sextic * (sq * sq))


def coefficient(par, kind, l, width=LANES):
    row = par[kind * LAYERS + l : kind * LAYERS + l + 1, 0:width]
    return row if kind > 3 else (4.0, 2.0, 6.0, DT)[kind] * row


def border_kernel(p_ref, al_ref, last_ref, buf, sems):
    copies = [
        pltpu.make_async_copy(src.at[:, pl.ds(ROWS - 8, 8), :], buf.at[cells], sems.at[k])
        for k, (src, cells) in enumerate(((p_ref, pl.ds(0, 24)), (al_ref, pl.ds(24, 8))))
    ]
    for copy in copies:
        copy.start()
    for copy in copies:
        copy.wait()
    for n in range(32):
        for r in range(4):
            last_ref[r * 32 + n : r * 32 + n + 1, :] = buf[n, 4 + r : 5 + r, :]


def rows_of(ref, c, l, low, high):
    if 0 <= l < LAYERS:
        n = c * LAYERS + l
        return ref[n * 40 + low : n * 40 + high, :]
    return jnp.zeros((high - low, LANES), F32)


def charges(px, nx, par, low, high, store):
    at = rows_of
    first, last = low - 1, high + 1
    for l in range(LAYERS):
        p = [at(px, c, l, first, last) for c in range(3)]
        total = p[0] * p[0] + p[1] * p[1] + p[2] * p[2]
        alpha2 = 2.0 * at(px, 3, l, first, last)
        e = coefficient(par, 3, l)
        landau = [coefficient(par, k, l) for k in range(3)]
        for c in range(3):
            drive = drive_of(p[c], alpha2, total, *landau)
            lap = (
                at(px, c, l, first + 1, last + 1) + at(px, c, l, first - 1, last - 1)
                + at(px, c, l + 1, first, last) + at(px, c, l - 1, first, last)
                - 6.0 * p[c]
            )
            n = c * LAYERS + l
            nx[n * 40 + first : n * 40 + last, :] = p[c] - DT * drive + e * lap
    lane = lax.broadcasted_iota(jnp.int32, (high - low, LANES), 1)
    for l in range(LAYERS):
        e = coefficient(par, 3, l)
        dx = -0.5 * (at(px, 0, l, low + 1, high + 1) - at(px, 0, l, low - 1, high - 1))
        above, below = at(px, 2, l + 1, low, high), at(px, 2, l - 1, low, high)
        p1, n1 = at(px, 1, l, low, high), at(nx, 1, l, low, high)
        fwd, bwd = shift(p1, -1), shift(p1, 1)
        one = dx - 0.5 * (above - below) - 0.5 * (fwd - bwd)
        wrap_one = jnp.where(lane == LANES - 1, -0.5 * fwd, jnp.where(lane == 0, 0.5 * bwd, 0.0))
        e_up = coefficient(par, 3, l + 1) if l + 1 < LAYERS else 0.0
        e_dn = coefficient(par, 3, l - 1) if l > 0 else 0.0
        ue = e * dx - 0.5 * (e_up * above - e_dn * below)
        un = -0.5 * (at(nx, 0, l, low + 1, high + 1) - at(nx, 0, l, low - 1, high - 1)) - 0.5 * (
            at(nx, 2, l + 1, low, high) - at(nx, 2, l - 1, low, high)
        )
        a = shift(ue - 0.5 * n1, -1)
        b = shift(ue + 0.5 * n1, 1)
        h = (0.5 * e) * p1
        c2, d2 = shift(h, -2), shift(h, 2)
        two = un + a + b - c2 + d2
        wrap_two = (
            jnp.where(lane == LANES - 1, a, 0.0)
            + jnp.where(lane == 0, b, 0.0)
            + jnp.where(lane >= LANES - 2, -c2, 0.0)
            + jnp.where(lane < 2, d2, 0.0)
        )
        store(0, l, one - wrap_one, wrap_one)
        store(1, l, two - wrap_two, wrap_two)


def stage_kernel(p_ref, al_ref, par, after, out_ref, head_ref, first_ref, px, nx, ws, eb):
    for n in range(32):
        ref, m = (p_ref, n) if n < 24 else (al_ref, n - 24)
        px[n * 40 + 8 : n * 40 + 40, :] = ref[m * ROWS : (m + 1) * ROWS, :]
        head_ref[n * 8 : (n + 1) * 8, :] = ref[m * ROWS : m * ROWS + 8, :]
        eb[n : n + 1, :] = pack(ref[m * ROWS : (m + 1) * ROWS, :])
    eb[32:48, :] = jnp.zeros((16, LANES), F32)
    for r in range(2):
        first_ref[r * 32 : (r + 1) * 32, :] = px[pl.ds(8 + r, 32, stride=40), :]

    def store(f, l, main, wrap):
        r = f * 16 + l
        out_ref[pl.ds(4 * SLOT + r, 12, stride=SLOT), :] = main[0:12]
        ws[pl.ds(4 * 32 + r, 12, stride=32), :] = wrap[0:12]
        out_ref[pl.ds(r + 8, NB, stride=SLOT), :] = main[12:28]
        ws[pl.ds(r + 8, NB, stride=32), :] = wrap[12:28]
        for b in range(4):
            ws[b * 32 + r : b * 32 + r + 1, :] = jnp.zeros((1, LANES), F32)
            out_ref[b * SLOT + r : b * SLOT + r + 1, :] = jnp.zeros((1, LANES), F32)

    charges(px, nx, par, 10, 38, store)
    blank = jnp.zeros((4, LANES), F32)
    for b in range(NB):
        out_ref[b * SLOT + 32 : (b + 1) * SLOT, :] = jnp.concatenate(
            [pack(ws[b * 32 : (b + 1) * 32, :]), eb[3 * b : 3 * b + 3, :], blank], axis=0
        )


def charge_kernel(part_ref, head_ref, lo_ref, par, tab, out_ref, px, nx, ws):
    out_ref[...] = part_ref[...]
    for n in range(32):
        px[n * 40 + 8 : n * 40 + 16, :] = head_ref[n * 8 : (n + 1) * 8, :]
    for r in range(4):
        px[pl.ds(4 + r, 32, stride=40), :] = lo_ref[r * 32 : (r + 1) * 32, :]
    ws[...] = jnp.zeros_like(ws)

    def store(f, l, main, wrap):
        r = f * 16 + l
        for b in range(4):
            out_ref[b * SLOT + r : b * SLOT + r + 1, :] = main[b : b + 1]
            ws[b * 32 + r : b * 32 + r + 1, :] = wrap[b : b + 1]

    charges(px, nx, par, 6, 10, store)
    for b in range(4):
        out_ref[b * SLOT + 32 : b * SLOT + 33, :] = part_ref[b * SLOT + 32 : b * SLOT + 33, :] + pack(
            ws[b * 32 : (b + 1) * 32, :]
        )
    at = (32 // 3) * SLOT + 33 + 32 % 3
    out_ref[at : at + 1, :] = pack(lo_ref[96:128, :])


def y_forward_kernel(in_ref, tab, tw, lo_ref, hi_ref, out_ref, corner_ref, d_ref, o_ref):
    corner_ref[...] = jnp.concatenate([pack(hi_ref[0:32, :]), jnp.zeros((7, LANES), F32)], axis=0)
    fh, fl, f0h, f0l = (tab[k * 256 : (k + 1) * 256, :] for k in range(4))
    lane1 = lax.broadcasted_iota(jnp.int32, (1, LANES), 1)
    lane = lax.broadcasted_iota(jnp.int32, (ROWS, LANES), 1)
    g = []
    for b in range(NB):
        before = in_ref[((b - 1) % NB) * SLOT + 32 : ((b - 1) % NB) * SLOT + 33, :]
        after = in_ref[((b + 1) % NB) * SLOT + 32 : ((b + 1) % NB) * SLOT + 33, :]
        extra = unpack(jnp.where(lane1 % 4 < 2, before, after))
        g.append(
            in_ref[b * SLOT : b * SLOT + 32, :]
            + jnp.where((lane < 2) | (lane >= 126), extra, 0.0)
        )
    plus = {b: g[b] + g[NB - b] for b in range(1, 8)}
    minus = {b: g[b] - g[NB - b] for b in range(1, 8)}
    re, im = {}, {}
    for k in range(5):
        even = g[0] + g[8] if k % 2 == 0 else g[0] - g[8]
        odd = jnp.zeros_like(even)
        s_even, s_odd = jnp.zeros_like(even), jnp.zeros_like(even)
        for b in range(1, 8):
            c, s = np.cos(2 * np.pi * b * k / 16), np.sin(2 * np.pi * b * k / 16)
            tc = plus[b] * float(c) if abs(c) > 1e-9 else None
            ts = minus[b] * float(s) if abs(s) > 1e-9 else None
            if b % 2 == 0:
                even = even + tc if tc is not None else even
                s_even = s_even + ts if ts is not None else s_even
            else:
                odd = odd + tc if tc is not None else odd
                s_odd = s_odd + ts if ts is not None else s_odd
        re[k], re[8 - k] = even + odd, even - odd
        im[k], im[8 - k] = -(s_even + s_odd), s_even - s_odd
    d_ref[0:32, 0:LANES] = re[0]
    d_ref[0:32, LANES:256] = re[8]
    for j in range(1, 8):
        c, s = tw[j : j + 1, :], tw[8 + j : 9 + j, :]
        d_ref[j * 32 : (j + 1) * 32, 0:LANES] = re[j] * c + im[j] * s
        d_ref[j * 32 : (j + 1) * 32, LANES:256] = im[j] * c - re[j] * s
    dh, dl = split(d_ref[...])
    o_ref[...] = dot_t(fh, dh) + dot_t(fh, dl) + dot_t(fl, dh)
    zero = dot_t(f0h, dh[0:128]) + dot_t(f0h, dl[0:128]) + dot_t(f0l, dh[0:128])
    wide = lax.broadcasted_iota(jnp.int32, (256, LANES), 1)
    o_ref[:, 0:LANES] = jnp.where(wide < 32, zero, o_ref[:, 0:LANES])
    lane64 = lax.broadcasted_iota(jnp.int32, (64, LANES), 1)
    for j in range(8):
        t, at = j // 4, j % 4
        value = None
        for q in range(4):
            piece = o_ref[q * 64 : (q + 1) * 64, t * LANES : (t + 1) * LANES]
            if q != at:
                piece = shift(piece, (q - at) * 32)
            value = piece if value is None else jnp.where(lane64 // 32 == q, piece, value)
        out_ref[j * 64 : (j + 1) * 64, :] = value


def x_kernel(in_ref, th, tl, lam, par, lo_ref, hi_ref, out_ref, zs, ys):
    n = in_ref.shape[0]
    half = n // 2
    top, low = in_ref[0:half, :], in_ref[half:n, :]
    for part, value in enumerate((top + low, top - low)):
        high, rest = split(value)
        both = jnp.concatenate([high, rest], axis=1)
        for chunk in range(n // 256):
            r0 = part * n + chunk * 256
            acc = []
            for xl in range(2):
                cols = slice(xl * half, (xl + 1) * half)
                wide = dot(th[r0 : r0 + 256, cols], both)
                acc.append(
                    wide[:, 0:LANES] + wide[:, LANES:256] + dot(tl[r0 : r0 + 256, cols], high)
                )
            turned = jnp.transpose(acc[0] + shift(acc[1], -8))
            zs[r0 : r0 + LANES, :] = turned[:, 0:LANES]
            zs[r0 + LANES : r0 + 256, :] = turned[:, LANES:256]
    dev = lax.axis_index("bx") * NB + lax.axis_index("by")
    j = dev // 64
    q = lax.broadcasted_iota(jnp.int32, (8, 1), 0) // 2
    s = q * 64 + dev % 64
    ky_j = j + 16 * (s % 128)
    ky_0 = jnp.where(s < 128, 16 * jnp.where(s <= 64, s, s - 64), 8 + 16 * (s % 64))
    ky = jnp.where(j == 0, ky_0, ky_j)
    full = NB * LANES
    ky = jnp.minimum(ky, full - ky).astype(F32)
    ky = jnp.broadcast_to(ky, (8, LANES))
    sin_half = jnp.sin(ky * (np.pi / full))
    lam_y = 4.0 * sin_half * sin_half
    sin_y = jnp.sin(jnp.minimum(ky, full // 2 - ky) * (2.0 * np.pi / full))
    slope_y = sin_y * sin_y
    second = lax.broadcasted_iota(jnp.int32, (8, LANES), 0) % 2 == 1
    eps = [coefficient(par, 4, l) for l in range(LAYERS)]
    iface = [coefficient(par, 5, l) for l in range(LAYERS + 1)]
    for chunk in range(2 * n // LANES):
        lateral = lam_y + lam[16 + chunk : 17 + chunk, :]
        slope = slope_y + lam[16 + 2 * n // LANES + chunk : 17 + 2 * n // LANES + chunk, :]
        inverse, ratio = [], []
        for l in range(LAYERS):
            pivot = eps[l] * lateral + (iface[l] + iface[l + 1])
            if l > 0:
                pivot = pivot - iface[l] * ratio[-1]
            inverse.append(1.0 / pivot)
            ratio.append(iface[l + 1] * inverse[-1])

        def solve(source):
            prime = []
            for l in range(LAYERS):
                value = source[l] + iface[l] * prime[-1] if l > 0 else source[l]
                prime.append(value * inverse[l])
            for l in range(LAYERS - 2, -1, -1):
                prime[l] = prime[l] + ratio[l] * prime[l + 1]
            return prime

        phi = solve([zs[pl.ds(chunk * LANES + l, 8, stride=16), :] for l in range(LAYERS)])
        first = [jnp.where(second, pltpu.roll(v, 1, axis=0), 0.0) for v in phi]
        zero = jnp.zeros_like(first[0])

        def dz(v):
            return [
                0.5 * ((v[l + 1] if l + 1 < LAYERS else zero) - (v[l - 1] if l > 0 else zero))
                for l in range(LAYERS)
            ]

        twice = dz(dz(first))
        more = solve([DT * (twice[l] - slope * first[l]) for l in range(LAYERS)])
        for l in range(LAYERS):
            value = phi[l] + more[l]
            ys[pl.ds(chunk * LANES + l, 8, stride=16), :] = value
            ys[pl.ds(chunk * LANES + 8 + l, 8, stride=16), :] = value
    odd_row = lax.broadcasted_iota(jnp.int32, (LANES, half), 0) // 8 % 2 == 1
    pair = []
    for part in range(2):
        high, rest = split(
            jnp.concatenate([ys[r : r + LANES, :] for r in range(part * n, (part + 1) * n, LANES)], axis=1)
        )
        rows = slice(part * n, (part + 1) * n)
        both = dot(jnp.concatenate([high, rest], axis=0), th[rows, :])
        both = both[0:LANES] + both[LANES:256] + dot(high, tl[rows, :])
        pair.append(jnp.where(odd_row, both[:, half:n], both[:, 0:half]))
    out_ref[0:half, :] = jnp.transpose(pair[0] + pair[1])
    out_ref[half:n, :] = jnp.transpose(pair[0] - pair[1])


def y_inverse_kernel(in_ref, tab, tw, lines, corner_ref, lo_ref, hi_ref, out_ref, o_ref):
    gh, gl, g0h, g0l = (tab[k * 256 : (k + 1) * 256, :] for k in range(4))
    lane64 = lax.broadcasted_iota(jnp.int32, (64, LANES), 1)
    for t in range(2):
        for q in range(4):
            value = None
            for at in range(4):
                j = t * 4 + at
                piece = in_ref[j * 64 : (j + 1) * 64, :]
                if q != at:
                    piece = shift(piece, (at - q) * 32)
                value = piece if value is None else jnp.where(lane64 // 32 == at, piece, value)
            o_ref[q * 64 : (q + 1) * 64, t * LANES : (t + 1) * LANES] = value
    oh, ol = split(o_ref[...])
    o_ref[...] = dot(gh, oh) + dot(gh, ol) + dot(gl, oh)
    zero = (
        dot(g0h, oh[:, 0:LANES]) + dot(g0h, ol[:, 0:LANES]) + dot(g0l, oh[:, 0:LANES])
    )
    wide = lax.broadcasted_iota(jnp.int32, (256, LANES), 1)
    o_ref[:, 0:LANES] = jnp.where(wide < 32, zero, o_ref[:, 0:LANES])
    g = jnp.transpose(o_ref[...])
    hr, hi = {}, {}
    for j in range(1, 8):
        c, s = tw[j : j + 1, :], tw[8 + j : 9 + j, :]
        a, b = g[j * 32 : (j + 1) * 32, 0:LANES], g[j * 32 : (j + 1) * 32, LANES:256]
        hr[j] = a * c - b * s
        hi[j] = a * s + b * c
    g0, g8 = g[0:32, 0:LANES], g[0:32, LANES:256]
    out = {}
    for b in range(5):
        even = g0 + g8 if b % 2 == 0 else g0 - g8
        odd = jnp.zeros_like(even)
        s_even, s_odd = jnp.zeros_like(even), jnp.zeros_like(even)
        for j in range(1, 8):
            c, s = np.cos(2 * np.pi * b * j / 16), np.sin(2 * np.pi * b * j / 16)
            tc = hr[j] * float(c) if abs(c) > 1e-9 else None
            ts = hi[j] * float(s) if abs(s) > 1e-9 else None
            if j % 2 == 0:
                even = even + tc if tc is not None else even
                s_even = s_even + ts if ts is not None else s_even
            else:
                odd = odd + tc if tc is not None else odd
                s_odd = s_odd + ts if ts is not None else s_odd
        cos_b, sin_b = even + odd, s_even + s_odd
        cos_c, sin_c = even - odd, s_odd - s_even
        out[b] = cos_b - sin_b
        out[(NB - b) % NB] = cos_b + sin_b
        out[8 - b] = cos_c - sin_c
        out[8 + b] = cos_c + sin_c
    lane = lax.broadcasted_iota(jnp.int32, (ROWS, LANES), 1)
    tail = corner_ref[0:4, :]
    from_right = lax.broadcasted_iota(jnp.int32, (3, LANES), 1) % 4 < 2
    for b in range(NB):
        after, before = (b + 1) % NB, (b - 1) % NB
        for k, r in enumerate((8, 24, 0, 16)):
            out_ref[b * SLOT + k * 8 : b * SLOT + (k + 1) * 8, :] = out[b][r : r + 8]
        border = jnp.where(lane < 2, out[after], out[before])
        edge = jnp.where(
            from_right,
            lines[after * SLOT + 33 : after * SLOT + 36, :],
            lines[before * SLOT + 33 : before * SLOT + 36, :],
        )
        out_ref[b * SLOT + 32 : (b + 1) * SLOT, :] = jnp.concatenate([pack(border), edge, tail], axis=0)


def wide(main, side, n, low, high):
    if n is None:
        return jnp.zeros((high - low, 2 * LANES), F32)
    rows = slice(n * 48 + low, n * 48 + high)
    return jnp.concatenate([main[rows, :], side[rows, :]], axis=1)


def edge_row(n):
    return n // 3 * SLOT + 33 + n % 3


def near(base, l):
    return base + l if 0 <= l < LAYERS else None


def layer_rows(ref, base, l, low, high):
    if 0 <= l < LAYERS:
        return ref[(base + l) * 48 + low : (base + l) * 48 + high, :]
    return jnp.zeros((high - low, LANES), F32)


def first_step(qm, qs, fm, fs, rm, rs, low, high):
    for l in range(LAYERS):
        phi = wide(fm, fs, l, low, high)
        slope = (
            wide(fm, fs, l, low + 1, high + 1) - wide(fm, fs, l, low - 1, high - 1),
            shift(phi, -1) - shift(phi, 1),
            wide(fm, fs, near(0, l + 1), low, high) - wide(fm, fs, near(0, l - 1), low, high),
        )
        for c in range(3):
            rows = slice((c * LAYERS + l) * 48 + low, (c * LAYERS + l) * 48 + high)
            rm[rows, :] = qm[rows, :] - (0.5 * DT) * slope[c][:, 0:LANES]
            rs[rows, :] = qs[rows, :] - (0.5 * DT) * slope[c][:, LANES : 2 * LANES]


def second_step(al_ref, fm, fs, rm, rs, par, low, high, store):
    at = layer_rows
    for l in range(LAYERS):
        p = [at(rm, c * LAYERS, l, low, high) for c in range(3)]
        total = p[0] * p[0] + p[1] * p[1] + p[2] * p[2]
        alpha2 = 2.0 * al_ref[l * ROWS + low - 8 : l * ROWS + high - 8, :]
        e = coefficient(par, 3, l)
        landau = [coefficient(par, k, l) for k in range(3)]
        phi = wide(fm, fs, LAYERS + l, low, high)
        field = (
            -0.5 * (at(fm, LAYERS, l, low + 1, high + 1) - at(fm, LAYERS, l, low - 1, high - 1)),
            -0.5 * (shift(phi, -1) - shift(phi, 1))[:, 0:LANES],
            -0.5 * (at(fm, LAYERS, l + 1, low, high) - at(fm, LAYERS, l - 1, low, high)),
        )
        for c in range(3):
            drive = drive_of(p[c], alpha2, total, *landau)
            both = wide(rm, rs, c * LAYERS + l, low, high)
            lap = (
                at(rm, c * LAYERS, l, low + 1, high + 1) + at(rm, c * LAYERS, l, low - 1, high - 1)
                + (shift(both, -1) + shift(both, 1))[:, 0:LANES]
                + at(rm, c * LAYERS, l + 1, low, high) + at(rm, c * LAYERS, l - 1, low, high)
                - 6.0 * p[c]
            )
            store(c * LAYERS + l, p[c] - DT * (drive - field[c]) + e * lap, field[c])


def star_kernel(p_ref, al_ref, lo_ref, hi_ref, phi_ref, par, qm, qs, pm, ps):
    from_right = lax.broadcasted_iota(jnp.int32, (1, LANES), 1) % 4 < 2
    by = lax.axis_index("by")
    left, right = (by + NB - 1) % NB, (by + 1) % NB
    corner_lo = unpack(phi_ref[edge_row(32) : edge_row(32) + 1, :])
    corner_hi = unpack(
        jnp.where(
            from_right, phi_ref[pl.ds(right * SLOT + 36, 1), :], phi_ref[pl.ds(left * SLOT + 36, 1), :]
        )
    )
    for n in range(32):
        ref, m = (p_ref, n) if n < 24 else (al_ref, n - 24)
        pm[n * 48 + 8 : n * 48 + 40, :] = ref[m * ROWS : (m + 1) * ROWS, :]
        ps[n * 48 + 8 : n * 48 + 40, :] = unpack(phi_ref[edge_row(n) : edge_row(n) + 1, :])
    for row, value, corner in (
        (6, lo_ref[64:96, :], corner_lo),
        (7, lo_ref[96:128, :], corner_lo),
        (40, hi_ref[0:32, :], corner_hi),
        (41, hi_ref[32:64, :], corner_hi),
    ):
        pm[pl.ds(row, 32, stride=48), :] = value
        ps[pl.ds(row, 32, stride=48), :] = corner
    for l in range(LAYERS):
        p = [wide(pm, ps, c * LAYERS + l, 7, 41) for c in range(3)]
        total = p[0] * p[0] + p[1] * p[1] + p[2] * p[2]
        alpha2 = 2.0 * wide(pm, ps, 24 + l, 7, 41)
        e = coefficient(par, 3, l, 2 * LANES)
        landau = [coefficient(par, k, l, 2 * LANES) for k in range(3)]
        for c in range(3):
            n = c * LAYERS + l
            drive = drive_of(p[c], alpha2, total, *landau)
            lap = (
                wide(pm, ps, n, 8, 42) + wide(pm, ps, n, 6, 40) + shift(p[c], -1) + shift(p[c], 1)
                + wide(pm, ps, near(c * LAYERS, l + 1), 7, 41)
                + wide(pm, ps, near(c * LAYERS, l - 1), 7, 41)
                - 6.0 * p[c]
            )
            value = p[c] - DT * drive + e * lap
            qm[n * 48 + 7 : n * 48 + 41, :] = value[:, 0:LANES]
            qs[n * 48 + 7 : n * 48 + 41, :] = value[:, LANES : 2 * LANES]


def inner_kernel(al_ref, qm, qs, phi_ref, par, out_ref, field_ref, fm, fs, rm, rs, ht):
    for src in range(NB):
        ht[src * 32 : (src + 1) * 32, :] = unpack(phi_ref[src * SLOT + 32 : src * SLOT + 33, :])
    for f in range(2):
        for l in range(LAYERS):
            for xl in range(2):
                r = f * 16 + xl * 8 + l
                row = (f * LAYERS + l) * 48 + 8 - SHIFT + xl * NB
                fm[row : row + NB, :] = phi_ref[pl.ds((1 - xl) * 16 + f * 8 + l, NB, stride=SLOT), :]
                fs[row : row + NB, :] = ht[pl.ds(r, NB, stride=32), :]
    first_step(qm, qs, fm, fs, rm, rs, 7, 33)

    def store(n, value, field):
        out_ref[n, 0:24, :] = value
        field_ref[n, 0:24, :] = field

    second_step(al_ref, fm, fs, rm, rs, par, 8, 32, store)


def update_kernel(
    al_ref, qm, qs, gm, gs, far_ref, par, out_in, field_in, out_ref, field_ref, fm, fs, rm, rs, to, tf, sems
):
    for n in range(2 * LAYERS):
        fm[n * 48 + 30 : n * 48 + 38, :] = gm[n * 48 + 30 : n * 48 + 38, :]
        fs[n * 48 + 30 : n * 48 + 38, :] = gs[n * 48 + 30 : n * 48 + 38, :]
    for k in range(4):
        side = unpack(far_ref[k * 24 + 16 : k * 24 + 17, :])
        for f in range(2):
            rows = pl.ds(f * LAYERS * 48 + 38 + k, LAYERS, stride=48)
            fm[rows, :] = far_ref[k * 24 + f * 8 : k * 24 + f * 8 + 8, :]
            fs[rows, :] = side[f * 16 : f * 16 + 8]
    first_step(qm, qs, fm, fs, rm, rs, 31, 41)

    def store(n, value, field):
        to[n] = value
        tf[n] = field

    second_step(al_ref, fm, fs, rm, rs, par, 32, 40, store)
    copies = [
        pltpu.make_async_copy(src, dst.at[:, pl.ds(24, 8), :], sems.at[k])
        for k, (src, dst) in enumerate(((to, out_ref), (tf, field_ref)))
    ]
    for copy in copies:
        copy.start()
    for copy in copies:
        copy.wait()


VMEM = pl.BlockSpec(memory_space=pltpu.VMEM)
ANY = pl.BlockSpec(memory_space=pl.ANY)


def call(kernel, shapes, specs, scratch, name, out=VMEM, aliases=None, dtype=None, mib=16):
    many = isinstance(shapes, list)
    return pl.pallas_call(
        kernel,
        out_shape=[jax.ShapeDtypeStruct(s, d) for s, d in zip(shapes, dtype or [F32] * len(shapes))]
        if many
        else jax.ShapeDtypeStruct(shapes, F32),
        in_specs=specs,
        out_specs=[out] * len(shapes) if many else out,
        input_output_aliases=aliases or {},
        scratch_shapes=[s if not isinstance(s, tuple) else pltpu.VMEM(s, F32) for s in scratch],
        compiler_params=pltpu.CompilerParams(vmem_limit_bytes=int(mib * 1024 * 1024)),
        cost_estimate=pl.CostEstimate(flops=0, transcendentals=0, bytes_accessed=int(3.5e6 * MICROSECONDS[name])),
        name=name,
    )


def shards(tabs, polarization, alpha_field, landau, stiffness, permittivity, interfaces):
    count = lax.axis_size("bx")
    devices = count * NB
    ahead = [(i, (i + 1) % count) for i in range(count)]
    behind = [(i, (i - 1) % count) for i in range(count)]
    cells = polarization.reshape(24 * ROWS, LANES)
    alpha = alpha_field.reshape(LAYERS * ROWS, LANES)
    par = jnp.concatenate([landau[0], landau[1], landau[2], stiffness, permittivity, interfaces])
    par = jnp.broadcast_to(par[:, None], (par.shape[0], 2 * LANES))
    last = call(
        border_kernel, (128, LANES), [ANY] * 2,
        [(32, 8, LANES), pltpu.SemaphoreType.DMA((2,))], "border", mib=53.8,
    )(polarization.reshape(24, ROWS, LANES), alpha_field)
    low = lax.ppermute(last, "bx", ahead)
    part, head, first = call(
        stage_kernel, [(NB * SLOT, LANES), (256, LANES), (64, LANES)], [VMEM] * 3 + [ANY],
        [(32 * 40, LANES), (24 * 40, LANES), (NB * 32, LANES), (48, LANES)], "stage",
    )(cells, alpha, par, last)
    high = lax.ppermute(first, "bx", behind)
    sent = call(
        charge_kernel, (NB * SLOT, LANES), [VMEM] * 4 + [ANY],
        [(32 * 40, LANES), (24 * 40, LANES), (4 * 32, LANES)], "charge",
    )(part, head, low, par, tabs["fwd"])
    lines = lax.all_to_all(sent.reshape(NB, SLOT, LANES), "by", 0, 0, tiled=True).reshape(NB * SLOT, LANES)
    modes, corner = call(
        y_forward_kernel, [(devices, LANES), (8, LANES)], [VMEM] * 5, [(256, 256)] * 2, "y_forward"
    )(lines, tabs["fwd"], tabs["small"], low, high)
    modes = lax.all_to_all(modes.reshape(devices, 1, LANES), ("bx", "by"), 0, 0, tiled=True)
    modes = call(
        x_kernel, (devices, LANES), [VMEM] * 7, [(2 * devices, LANES)] * 2, "x_solve"
    )(modes.reshape(devices, LANES), *tabs["x"], tabs["small"], par, low, high)
    modes = lax.all_to_all(modes.reshape(devices, 1, LANES), ("bx", "by"), 0, 0, tiled=True)
    sent = call(
        y_inverse_kernel, (NB * SLOT, LANES), [VMEM] * 7, [(256, 256)], "y_inverse"
    )(modes.reshape(devices, LANES), tabs["inv"], tabs["small"], lines, corner, low, high)
    phi = lax.all_to_all(sent.reshape(NB, SLOT, LANES), "by", 0, 0, tiled=True)
    far = lax.ppermute(phi[:4, 16:].reshape(4 * 24, LANES), "bx", behind)
    phi = phi.reshape(NB * SLOT, LANES)
    star = call(
        star_kernel, [(24 * 48, LANES)] * 2, [VMEM] * 6, [(32 * 48, LANES)] * 2, "star",
    )(cells, alpha, low, high, phi, par)
    polar, field, *grid = call(
        inner_kernel, [(24, ROWS, LANES)] * 2 + [(16 * 48, LANES)] * 2, [VMEM] * 5,
        [(24 * 48, LANES)] * 2 + [(NB * 32, LANES)], "inner",
    )(alpha, *star, phi, par)
    polar, field = call(
        update_kernel, [(24, ROWS, LANES)] * 2, [VMEM] * 7 + [ANY] * 2,
        [(16 * 48, LANES)] * 2 + [(24 * 48, LANES)] * 2 + [(24, 8, LANES)] * 2 + [pltpu.SemaphoreType.DMA((2,))],
        "update", out=ANY, aliases={7: 0, 8: 1},
    )(alpha, *star, *grid, far, par, polar, field)
    return polar.reshape(polarization.shape), field.reshape(polarization.shape)


def solution(mesh):
    fwd, fwd0, inv, inv0, tw = tables_y()
    table, lam = tables_x(mesh.shape["bx"] * ROWS, -SHIFT)
    tabs = {
        "fwd": np.concatenate([*split_table(fwd), *split_table(fwd0)], axis=0),
        "inv": np.concatenate([*split_table(inv), *split_table(inv0)], axis=0),
        "x": split_table(table),
        "small": np.concatenate([tw, lam], axis=0),
    }
    return jax.shard_map(
        functools.partial(shards, tabs),
        mesh=mesh,
        in_specs=(P(None, None, "bx", "by"), P(None, "bx", "by"), P(), P(), P(), P()),
        out_specs=(P(None, None, "bx", "by"), P(None, None, "bx", "by")),
        check_vma=False,
    )
```
